32 devices in a mesh: row: 4 (over z), col: 8 (over y, x, core).
Axes of the slice: x: 2, y: 2, z: 4, core: 2. Of those that a mesh axis runs over, the one named last changes fastest.
Arguments:
- vertices: float32 [3, 3840], P(None, ('row', 'col')), may hold values from -6 to 6
- connect: int32 [4, 3840], P(None, ('row', 'col')), may hold values from 0 to 119
- component: int32 [3840], P(('row', 'col')), may hold values from 0 to 4
- azimuth: float32 [1], replicated, may hold values from 0 to 6.2831
- adjoint_rhs: float32 [24, 3840], P(None, ('row', 'col')), may hold values from -6 to 6
Outputs:
- solution: float32 [24, 3840], P(None, ('row', 'col'))
- residual_sq: float32 [24], replicated
The draws below stay inside these ranges and needn't reach their ends.
Inputs may be any that keep to these rules, and one draw needn't show every extreme that they name: Entry connect[k, p] names vertex (p // 120) * 120 + connect[k, p], a vertex of the panel's own block. `component`: 0 marks a panel of the airframe body, b > 0 a panel of blade b.
All inputs are finite; a program needn't handle non-finite values.
Results may differ from the reference program's by a relative error of at most 0.0003.
Values sent between devices are 32-bit elements; how exact they have to be, the bound alone decides.
A program may use at most 64 MiB of HBM per device.

```python
import math
import jax
import jax.numpy as jnp
from jax import lax

UNIT = 120
RHS = 24
BLADES = 4
ORDER = 3840


def set_ends(drawn, key, low, largest):
    longest = drawn.shape.index(max(drawn.shape))
    spots = []
    for shift in (0, 1):
        where = [jax.random.randint(jax.random.fold_in(key, axis), (), 0, length) for axis, length in enumerate(drawn.shape)]
        where[longest] = (where[longest] + shift) % drawn.shape[longest]
        spots.append(tuple(where))
    return drawn.at[spots[0]].set(low).at[spots[1]].set(largest)


def block_levels(stream_key, extent, pieces, least, largest):
    def one(axis_at, parts):
        steps = jax.random.uniform(jax.random.fold_in(jax.random.fold_in(stream_key, 6), axis_at), (parts,), jnp.float32, least / len(pieces), largest / len(pieces))
        return jnp.repeat(jnp.exp(steps), extent[axis_at] // parts).reshape((-1,) + (1,) * (len(extent) - axis_at - 1))

    gain = one(*pieces[0])
    for cut in pieces[1:]:
        gain = gain * one(*cut)
    return gain


def gaussian(stream_key, shape, width, reach, pieces=(), held_as=jnp.bfloat16):
    drawn = width * jax.random.normal(stream_key, shape, jnp.float32)
    if pieces:
        drawn = drawn * block_levels(stream_key, shape, pieces, -0.22, 0.18)
    return jnp.clip(drawn, -reach, reach).astype(held_as)


def setup_inputs(seed: int = 0) -> dict:
    key_list = jax.random.split(jax.random.key(seed), 6)
    vertices = gaussian(key_list[0], (3, ORDER), 1.0, 6.0, ((1, 32),), jnp.float32)
    connect = set_ends(jax.random.randint(key_list[1], (4, ORDER), 0, UNIT), jax.random.fold_in(key_list[1], 1), 0, UNIT - 1).astype(jnp.int32)
    component = set_ends(jax.random.randint(key_list[2], (ORDER,), 0, BLADES + 1), jax.random.fold_in(key_list[2], 1), 0, BLADES).astype(jnp.int32)
    azimuth = jnp.clip(jax.random.uniform(key_list[3], (1,), jnp.float32, 0.0, 6.2831), 0.0, 6.2831)
    adjoint_rhs = gaussian(key_list[4], (RHS, ORDER), 1.0, 6.0, ((1, 32),), jnp.float32)
    return {"vertices": vertices, "connect": connect, "component": component, "azimuth": azimuth, "adjoint_rhs": adjoint_rhs}


epsilon = 1e-06
core_square = 0.04
highest = lax.Precision.HIGHEST

def panel_frame(corners, component, azimuth, blades):
    angle_turn = azimuth[0] + 2.0 * math.pi / blades * (component - 1).astype(jnp.float32)
    cosine = jnp.cos(angle_turn)[None, :]
    sine_turn = jnp.sin(angle_turn)[None, :]
    on_rotor = (component > 0)[None, :]
    xcoord = corners[0]
    ycoord = corners[1]
    turned_x = jnp.where(on_rotor, cosine * xcoord - sine_turn * ycoord, xcoord)
    turned_y = jnp.where(on_rotor, sine_turn * xcoord + cosine * ycoord, ycoord)
    placed = jnp.stack([turned_x, turned_y, corners[2]])
    centers = lax.optimization_barrier(jnp.mean(placed, axis=1))
    diagonal_one = placed[:, 2] - placed[:, 0]
    diagonal_two = placed[:, 3] - placed[:, 1]
    areas = 0.5 * jnp.stack([diagonal_one[1] * diagonal_two[2] - diagonal_one[2] * diagonal_two[1], diagonal_one[2] * diagonal_two[0] - diagonal_one[0] * diagonal_two[2], diagonal_one[0] * diagonal_two[1] - diagonal_one[1] * diagonal_two[0]])
    return jnp.concatenate([centers, areas], axis=0)

def influence(receivers, sources, scale):
    delta_x = receivers[0][:, None] - sources[0][None, :]
    delta_y = receivers[1][:, None] - sources[1][None, :]
    delta_z = receivers[2][:, None] - sources[2][None, :]
    inverse = lax.rsqrt(delta_x * delta_x + delta_y * delta_y + delta_z * delta_z + core_square)
    doublet = (sources[3][None, :] * delta_x + sources[4][None, :] * delta_y + sources[5][None, :] * delta_z) * (inverse * inverse * inverse)
    return scale * (doublet + sources[5][None, :] * inverse)

def small_solve(start_norm, first_diag, first_sub, second_top, second_diag, second_sub):
    det_value = second_sub * second_sub * (first_diag * first_diag + first_sub * first_sub) + (first_diag * second_diag - first_sub * second_top) ** 2
    gram_00 = first_diag * first_diag + first_sub * first_sub
    gram_01 = first_diag * second_top + first_sub * second_diag
    gram_11 = second_top * second_top + second_diag * second_diag + second_sub * second_sub
    coef_one = start_norm * (gram_11 * first_diag - gram_01 * second_top) / det_value
    coef_two = start_norm * (gram_00 * second_top - gram_01 * first_diag) / det_value
    error_one = start_norm - first_diag * coef_one - second_top * coef_two
    error_two = -first_sub * coef_one - second_diag * coef_two
    error_three = -second_sub * coef_two
    return (coef_one, coef_two, error_one * error_one + error_two * error_two + error_three * error_three)

def reference(vertices, connect, component, azimuth, adjoint_rhs):
    order = vertices.shape[1]
    panel = jnp.arange(order, dtype=jnp.int32)
    base_index = panel // UNIT * UNIT
    corners = vertices[:, (base_index[None, :] + connect).astype(jnp.int32)]
    frames = panel_frame(corners, component, azimuth, BLADES)
    diag_term = 3.0 + jnp.sqrt(lax.optimization_barrier(jnp.sum(frames[3:] * frames[3:], axis=0)))
    scale = 2.0 / math.sqrt(order)
    block_rows = UNIT * 4
    block_count = order // block_rows

    def apply_matrix(vector):

        def step_block(block_index, total):
            begin = (block_index * block_rows).astype(jnp.int32)
            receivers = lax.dynamic_slice_in_dim(frames, begin, block_rows, 1)
            piece = lax.dynamic_slice_in_dim(vector, begin, block_rows, 1)
            return total + jnp.dot(piece, influence(receivers, frames, scale), precision=highest, preferred_element_type=jnp.float32)
        summed = lax.fori_loop(0, block_count, step_block, jnp.zeros(vector.shape, jnp.float32))
        return summed + diag_term[None, :] * vector
    rhs_value = adjoint_rhs
    start_norm = jnp.sqrt(lax.optimization_barrier(jnp.sum(rhs_value * rhs_value, axis=1)) + epsilon)
    basis_one = rhs_value / start_norm[:, None]
    image_one = apply_matrix(basis_one)
    first_diag = lax.optimization_barrier(jnp.sum(basis_one * image_one, axis=1))
    ortho_one = image_one - first_diag[:, None] * basis_one
    first_sub = jnp.sqrt(lax.optimization_barrier(jnp.sum(ortho_one * ortho_one, axis=1)) + epsilon)
    basis_two = ortho_one / first_sub[:, None]
    image_two = apply_matrix(basis_two)
    second_top = lax.optimization_barrier(jnp.sum(basis_one * image_two, axis=1))
    second_diag = lax.optimization_barrier(jnp.sum(basis_two * image_two, axis=1))
    ortho_two = image_two - second_top[:, None] * basis_one - second_diag[:, None] * basis_two
    second_sub = jnp.sqrt(lax.optimization_barrier(jnp.sum(ortho_two * ortho_two, axis=1)) + epsilon)
    coef_one, coef_two, residual_sq = small_solve(start_norm, first_diag, first_sub, second_top, second_diag, second_sub)
    solution = coef_one[:, None] * basis_one + coef_two[:, None] * basis_two
    return (solution, residual_sq)
```

```python
import functools
import math

import jax
import jax.numpy as jnp
from jax import lax
from jax.experimental import pallas as pl
from jax.experimental.pallas import tpu as pltpu
from jax.sharding import PartitionSpec as P

BLADES = 4
LANES = 128
SUB = 32

epsilon = 1e-06
core_square = 0.04
shift = 3.0


def panel_frame(corners, component, azimuth, blades):
    angle_turn = azimuth + 2.0 * math.pi / blades * (component - 1).astype(jnp.float32)
    cosine = jnp.cos(angle_turn)
    sine = jnp.sin(angle_turn)
    on_rotor = component > 0
    placed = []
    for corner in corners:
        x, y, z = corner[0:1], corner[1:2], corner[2:3]
        placed.append(
            (
                jnp.where(on_rotor, cosine * x - sine * y, x),
                jnp.where(on_rotor, sine * x + cosine * y, y),
                z,
            )
        )
    center = [
        (placed[0][k] + placed[1][k] + placed[2][k] + placed[3][k]) * 0.25 for k in range(3)
    ]
    one = [placed[2][k] - placed[0][k] for k in range(3)]
    two = [placed[3][k] - placed[1][k] for k in range(3)]
    area = [
        0.5 * (one[1] * two[2] - one[2] * two[1]),
        0.5 * (one[2] * two[0] - one[0] * two[2]),
        0.5 * (one[0] * two[1] - one[1] * two[0]),
    ]
    return center, area


def small_solve(gg, p1, p2, q0, q1, q2):
    n2 = gg + epsilon
    start_norm = jnp.sqrt(n2)
    one_one = gg / n2
    first_diag = p1 / n2 + shift * one_one
    sigma = (p1 - shift * epsilon) / n2
    uu = jnp.maximum((p2 - 2.0 * sigma * p1 + sigma * sigma * gg) / n2, 0.0)
    sub2 = uu + epsilon
    first_sub = jnp.sqrt(sub2)
    one_two = (p1 + shift * gg) * (epsilon / n2) / (n2 * first_sub)
    t0 = (q0 - sigma * p1) / (n2 * first_sub)
    second_top = t0 + shift * one_two
    two_two = uu / sub2
    t1 = (q1 - sigma * (p2 + q0 - sigma * p1)) / (n2 * sub2)
    second_diag = t1 + shift * two_two
    tau = t1 - shift * epsilon / sub2
    yy = (q2 - sigma * (2.0 * q1 - sigma * p2)) / (n2 * sub2)
    vv = (
        yy
        - 2.0 * (second_top * t0 + tau * t1)
        + second_top * second_top * one_one
        + tau * tau * two_two
        + 2.0 * second_top * tau * one_two
    )
    second_sub = jnp.sqrt(jnp.maximum(vv, 0.0) + epsilon)
    gram_00 = first_diag * first_diag + first_sub * first_sub
    cross = first_diag * second_diag - first_sub * second_top
    det_value = second_sub * second_sub * gram_00 + cross * cross
    gram_01 = first_diag * second_top + first_sub * second_diag
    gram_11 = second_top * second_top + second_diag * second_diag + second_sub * second_sub
    coef_one = start_norm * (gram_11 * first_diag - gram_01 * second_top) / det_value
    coef_two = start_norm * (gram_00 * second_top - gram_01 * first_diag) / det_value
    error_one = start_norm - first_diag * coef_one - second_top * coef_two
    error_two = -first_sub * coef_one - second_diag * coef_two
    error_three = -second_sub * coef_two
    residual = error_one * error_one + error_two * error_two + error_three * error_three
    of_w1 = coef_two / (start_norm * first_sub)
    of_g = coef_one / start_norm - sigma * of_w1
    return of_g, of_w1, residual


def split(value):
    twice = jnp.concatenate([value, value], axis=0)
    lead = twice.astype(jnp.bfloat16).astype(jnp.float32)
    row = lax.broadcasted_iota(jnp.int32, twice.shape, 0)
    return jnp.where(row < value.shape[0], lead, twice - lead).astype(jnp.bfloat16)


def kernel(
    nr, nc, width, rhs,
    azimuth_ref, vertices_ref, connect_ref, component_ref, rhs_ref,
    solution_ref, residual_ref,
    pad_f, pad_i, frames_col, frames_row, vec_col, image_col, halves, matrix,
    send_one, recv_one, send_two, recv_two, total_col, total_row,
    sems_fc, sems_fr, sems_g, sems_w, sems_one, sems_two, sems_tc, sems_tr,
):
    my_r, my_c = lax.axis_index("row"), lax.axis_index("col")
    scale = 2.0 / math.sqrt(width * nr * nc)
    cols = [lax.rem(my_c + k, nc) for k in range(1, nc)]
    rows = [lax.rem(my_r + k, nr) for k in range(1, nr)]

    barrier = pltpu.get_barrier_semaphore()
    for c in cols:
        pl.semaphore_signal(
            barrier, inc=1, device_id=(my_r, c), device_id_type=pl.DeviceIdType.MESH
        )
    for r in rows:
        pl.semaphore_signal(
            barrier, inc=1, device_id=(r, my_c), device_id_type=pl.DeviceIdType.MESH
        )

    started = []

    def push(source, target, sems, at_send, at_recv, device):
        copy = pltpu.make_async_remote_copy(
            src_ref=source,
            dst_ref=target,
            send_sem=sems.at[0, at_send],
            recv_sem=sems.at[1, at_recv],
            device_id=device,
            device_id_type=pl.DeviceIdType.MESH,
        )
        copy.start()
        started.append(copy)

    def to_plane(ref, sems):
        for c in cols:
            push(ref.at[my_c], ref.at[my_c], sems, c, my_c, (my_r, c))

    def to_line(source, ref, sems):
        for r in rows:
            at = my_r if source is None else r
            push((ref if source is None else source).at[at], ref.at[my_r], sems, r, my_r, (r, my_c))

    def arrived(ref, sems, at):
        pltpu.make_async_remote_copy(
            src_ref=ref.at[at],
            dst_ref=ref.at[at],
            send_sem=sems.at[0, at],
            recv_sem=sems.at[1, at],
            device_id=(my_r, my_c),
            device_id_type=pl.DeviceIdType.MESH,
        ).wait_recv()

    pad_f[...] = jnp.zeros_like(pad_f)
    pad_i[...] = jnp.zeros_like(pad_i)
    pad_f[0:3, 0:width] = vertices_ref[...]
    pad_i[0:4, 0:width] = connect_ref[...]
    pad_i[4:5, 0:width] = component_ref[...]
    vec_col[my_c] = jnp.zeros((rhs, LANES), jnp.float32)
    vec_col[my_c, :, 0:width] = rhs_ref[...]
    vertices = pad_f[...]
    corners = [
        jnp.take_along_axis(
            vertices,
            jnp.broadcast_to(pad_i[k : k + 1, :], vertices.shape),
            axis=1,
            mode="promise_in_bounds",
        )
        for k in range(4)
    ]
    center, area = panel_frame(corners, pad_i[4:5, :], azimuth_ref[0], BLADES)
    size = jnp.sqrt(area[0] * area[0] + area[1] * area[1] + area[2] * area[2])
    frame = jnp.concatenate(
        center + [scale * part for part in area] + [jnp.zeros((2, LANES), jnp.float32)], axis=0
    )
    frames_col[my_c] = frame
    frames_row[my_r] = frame

    pl.semaphore_wait(barrier, nc - 1 + nr - 1)
    to_line(None, frames_row, sems_fr)
    to_plane(frames_col, sems_fc)
    to_plane(vec_col, sems_g)

    def fill(c):
        columns = frames_col[c].T
        for s in range(LANES // SUB):
            x, y, z = (
                jnp.broadcast_to(columns[s * SUB : (s + 1) * SUB, k : k + 1], (SUB, LANES))
                for k in range(3)
            )
            place = pl.ds(pl.multiple_of(c * LANES + s * SUB, SUB), SUB)

            def one(r, carry):
                source = frames_row[r]
                dx, dy, dz = x - source[0:1], y - source[1:2], z - source[2:3]
                inverse = lax.rsqrt(dx * dx + dy * dy + (dz * dz + core_square))
                along = source[3:4] * dx + source[4:5] * dy + source[5:6] * dz
                value = inverse * (along * (inverse * inverse) + source[5:6])
                lead = value.astype(jnp.bfloat16)
                where = pl.ds(r * LANES if isinstance(r, int) else pl.multiple_of(r * LANES, LANES), LANES)
                matrix[0, place, where] = lead
                matrix[1, place, where] = (value - lead.astype(jnp.float32)).astype(jnp.bfloat16)
                return carry

            if nr <= 4:
                for r in range(nr):
                    one(r, 0)
            else:
                lax.fori_loop(0, nr, one, 0)

    def fill_step(k, carry):
        c = lax.rem(my_c + k, nc)
        arrived(frames_col, sems_fc, c)
        fill(c)
        return carry

    for r in rows:
        arrived(frames_row, sems_fr, r)
    fill(my_c)
    lax.fori_loop(1, nc, fill_step, 0)

    def place_halves(ref, c):
        halves[:, pl.ds(pl.multiple_of(c * LANES, LANES), LANES)] = split(ref[c])

    deep = min(nc, 8) * LANES

    def product(send, recv):
        def part(k):
            at = pl.ds(k * deep if isinstance(k, int) else pl.multiple_of(k * deep, deep), deep)
            return jnp.dot(
                halves[:, at], matrix[0, at, :], preferred_element_type=jnp.float32
            ) + jnp.dot(halves[:, at], matrix[1, at, :], preferred_element_type=jnp.float32)

        total = part(0)
        if nc * LANES > deep:
            total = lax.fori_loop(1, nc * LANES // deep, lambda k, t: t + part(k), total)
        total = total[:rhs] + total[rhs:]
        for r in range(nr):
            send[r] = total[:, r * LANES : (r + 1) * LANES]

    def apply_matrix(ref, send, recv, sems):
        product(send, recv)
        to_line(send, recv, sems)
        summed = send[my_r] + size * ref[my_c]
        for r in rows:
            arrived(recv, sems, r)
            summed = summed + recv[r]
        return summed

    place_halves(vec_col, my_c)
    for c in cols:
        arrived(vec_col, sems_g, c)
        place_halves(vec_col, c)
    w1 = apply_matrix(vec_col, send_one, recv_one, sems_one)
    image_col[my_c] = w1
    to_plane(image_col, sems_w)
    g = vec_col[my_c]
    lane = lax.broadcasted_iota(jnp.int32, (rhs, LANES), 1)

    def with_sum(tile, at, product):
        return jnp.where(lane == at, jnp.sum(product, axis=1, keepdims=True), tile)

    tile = jnp.zeros((rhs, LANES), jnp.float32)
    tile = with_sum(tile, 0, g * g)
    tile = with_sum(tile, 1, g * w1)
    tile = with_sum(tile, 2, w1 * w1)
    place_halves(image_col, my_c)
    for c in cols:
        arrived(image_col, sems_w, c)
        place_halves(image_col, c)
    w2 = apply_matrix(image_col, send_two, recv_two, sems_two)
    tile = with_sum(tile, 3, g * w2)
    tile = with_sum(tile, 4, w1 * w2)
    tile = with_sum(tile, 5, w2 * w2)

    total_col[my_c] = jnp.zeros((8, LANES), jnp.float32)
    total_col[my_c, :, 0:rhs] = tile.T[0:8, :]
    to_plane(total_col, sems_tc)
    for c in cols:
        arrived(total_col, sems_tc, c)
    total = total_col[0]
    for c in range(1, nc):
        total = total + total_col[c]
    total_row[my_r] = total
    to_line(None, total_row, sems_tr)
    for r in rows:
        arrived(total_row, sems_tr, r)
    total = total_row[0]
    for r in range(1, nr):
        total = total + total_row[r]
    of_g, of_w1, residual = small_solve(*(total[k : k + 1] for k in range(6)))
    residual_ref[...] = residual[:, 0:rhs]
    factors = jnp.concatenate([of_g, of_w1, jnp.zeros((6, LANES), jnp.float32)], axis=0).T
    answer = factors[0:rhs, 0:1] * g + factors[0:rhs, 1:2] * w1
    solution_ref[...] = answer[:, 0:width]
    for copy in started:
        copy.wait_send()


def on_device(nr, nc, vertices, connect, component, azimuth, adjoint_rhs):
    rhs, width = adjoint_rhs.shape
    vmem = pl.BlockSpec(memory_space=pltpu.VMEM)
    f32 = jnp.float32
    matrix_bytes = 2 * nc * nr * LANES * LANES * 2
    pair = lambda n: pltpu.SemaphoreType.DMA((2, n))
    answer, residual = pl.pallas_call(
        functools.partial(kernel, nr, nc, width, rhs),
        out_shape=(
            jax.ShapeDtypeStruct((rhs, width), f32),
            jax.ShapeDtypeStruct((1, rhs), f32),
        ),
        in_specs=[pl.BlockSpec(memory_space=pltpu.SMEM)] + [vmem] * 4,
        out_specs=(vmem, vmem),
        scratch_shapes=[
            pltpu.VMEM((8, LANES), f32),
            pltpu.VMEM((8, LANES), jnp.int32),
            pltpu.VMEM((nc, 8, LANES), f32),
            pltpu.VMEM((nr, 8, LANES), f32),
            pltpu.VMEM((nc, rhs, LANES), f32),
            pltpu.VMEM((nc, rhs, LANES), f32),
            pltpu.VMEM((2 * rhs, nc * LANES), jnp.bfloat16),
            pltpu.VMEM((2, nc * LANES, nr * LANES), jnp.bfloat16),
            pltpu.VMEM((nr, rhs, LANES), f32),
            pltpu.VMEM((nr, rhs, LANES), f32),
            pltpu.VMEM((nr, rhs, LANES), f32),
            pltpu.VMEM((nr, rhs, LANES), f32),
            pltpu.VMEM((nc, 8, LANES), f32),
            pltpu.VMEM((nr, 8, LANES), f32),
            pair(nc), pair(nr), pair(nc), pair(nc), pair(nr), pair(nr), pair(nc), pair(nr),
        ],
        compiler_params=pltpu.CompilerParams(
            collective_id=0,
            has_side_effects=True,
            vmem_limit_bytes=matrix_bytes + 20 * 1024 * 1024,
        ),
        cost_estimate=pl.CostEstimate(
            flops=2 * matrix_bytes * rhs, bytes_accessed=4 * rhs * width * 3, transcendentals=0
        ),
    )(azimuth, vertices, connect, component.reshape(1, width), adjoint_rhs)
    return answer, residual.reshape(rhs)


def solution(mesh):
    in_specs = (
        P(None, ("row", "col")),
        P(None, ("row", "col")),
        P(("row", "col")),
        P(),
        P(None, ("row", "col")),
    )
    out_specs = (P(None, ("row", "col")), P())
    return jax.shard_map(
        functools.partial(on_device, mesh.shape["row"], mesh.shape["col"]),
        mesh=mesh,
        in_specs=in_specs,
        out_specs=out_specs,
        check_vma=False,
    )
```

```python
import functools
import math

import jax
import jax.numpy as jnp
from jax import lax
from jax.experimental import pallas as pl
from jax.experimental.pallas import tpu as pltpu
from jax.sharding import PartitionSpec as P

BLADES = 4
LANES = 128
SUB = 32

epsilon = 1e-06
core_square = 0.04
shift = 3.0


def panel_frame(corners, component, azimuth, blades):
    angle_turn = azimuth + 2.0 * math.pi / blades * (component - 1).astype(jnp.float32)
    cosine = jnp.cos(angle_turn)
    sine = jnp.sin(angle_turn)
    on_rotor = component > 0
    placed = []
    for corner in corners:
        x, y, z = corner[0:1], corner[1:2], corner[2:3]
        placed.append(
            (
                jnp.where(on_rotor, cosine * x - sine * y, x),
                jnp.where(on_rotor, sine * x + cosine * y, y),
                z,
            )
        )
    center = [
        (placed[0][k] + placed[1][k] + placed[2][k] + placed[3][k]) * 0.25 for k in range(3)
    ]
    one = [placed[2][k] - placed[0][k] for k in range(3)]
    two = [placed[3][k] - placed[1][k] for k in range(3)]
    area = [
        0.5 * (one[1] * two[2] - one[2] * two[1]),
        0.5 * (one[2] * two[0] - one[0] * two[2]),
        0.5 * (one[0] * two[1] - one[1] * two[0]),
    ]
    return center, area


def small_solve(gg, p1, p2, q0, q1, q2):
    n2 = gg + epsilon
    start_norm = jnp.sqrt(n2)
    one_one = gg / n2
    first_diag = p1 / n2 + shift * one_one
    sigma = (p1 - shift * epsilon) / n2
    uu = jnp.maximum((p2 - 2.0 * sigma * p1 + sigma * sigma * gg) / n2, 0.0)
    sub2 = uu + epsilon
    first_sub = jnp.sqrt(sub2)
    one_two = (p1 + shift * gg) * (epsilon / n2) / (n2 * first_sub)
    t0 = (q0 - sigma * p1) / (n2 * first_sub)
    second_top = t0 + shift * one_two
    two_two = uu / sub2
    t1 = (q1 - sigma * (p2 + q0 - sigma * p1)) / (n2 * sub2)
    second_diag = t1 + shift * two_two
    tau = t1 - shift * epsilon / sub2
    yy = (q2 - sigma * (2.0 * q1 - sigma * p2)) / (n2 * sub2)
    vv = (
        yy
        - 2.0 * (second_top * t0 + tau * t1)
        + second_top * second_top * one_one
        + tau * tau * two_two
        + 2.0 * second_top * tau * one_two
    )
    second_sub = jnp.sqrt(jnp.maximum(vv, 0.0) + epsilon)
    gram_00 = first_diag * first_diag + first_sub * first_sub
    cross = first_diag * second_diag - first_sub * second_top
    det_value = second_sub * second_sub * gram_00 + cross * cross
    gram_01 = first_diag * second_top + first_sub * second_diag
    gram_11 = second_top * second_top + second_diag * second_diag + second_sub * second_sub
    coef_one = start_norm * (gram_11 * first_diag - gram_01 * second_top) / det_value
    coef_two = start_norm * (gram_00 * second_top - gram_01 * first_diag) / det_value
    error_one = start_norm - first_diag * coef_one - second_top * coef_two
    error_two = -first_sub * coef_one - second_diag * coef_two
    error_three = -second_sub * coef_two
    residual = error_one * error_one + error_two * error_two + error_three * error_three
    of_w1 = coef_two / (start_norm * first_sub)
    of_g = coef_one / start_norm - sigma * of_w1
    return of_g, of_w1, residual


def split(value):
    twice = jnp.concatenate([value, value], axis=0)
    lead = twice.astype(jnp.bfloat16).astype(jnp.float32)
    row = lax.broadcasted_iota(jnp.int32, twice.shape, 0)
    return jnp.where(row < value.shape[0], lead, twice - lead).astype(jnp.bfloat16)


def kernel(
    nr, nc, width, rhs,
    azimuth_in, vertices_in, connect_in, component_in, rhs_in,
    solution_ref, residual_ref,
    azimuth_ref, vertices_ref, connect_ref, component_ref, rhs_ref, sems_in,
    pad_f, pad_i, frames_col, frames_row, vec_col, image_col, halves, matrix,
    send_one, recv_one, send_two, recv_two, total_col, total_row,
    sems_fc, sems_fr, sems_g, sems_w, sems_one, sems_two, sems_tc, sems_tr,
):
    my_r, my_c = lax.axis_index("row"), lax.axis_index("col")
    scale = 2.0 / math.sqrt(width * nr * nc)
    cols = [lax.rem(my_c + k, nc) for k in range(1, nc)]
    rows = [lax.rem(my_r + k, nr) for k in range(1, nr)]

    loads = [
        pltpu.make_async_copy(source, target, sems_in.at[k])
        for k, (source, target) in enumerate(
            (
                (azimuth_in, azimuth_ref),
                (vertices_in, vertices_ref),
                (connect_in, connect_ref),
                (component_in, component_ref),
                (rhs_in, rhs_ref),
            )
        )
    ]
    for load in loads:
        load.start()
    barrier = pltpu.get_barrier_semaphore()
    for c in cols:
        pl.semaphore_signal(
            barrier, inc=1, device_id=(my_r, c), device_id_type=pl.DeviceIdType.MESH
        )
    for r in rows:
        pl.semaphore_signal(
            barrier, inc=1, device_id=(r, my_c), device_id_type=pl.DeviceIdType.MESH
        )

    started = []

    def push(source, target, sems, at_send, at_recv, device):
        copy = pltpu.make_async_remote_copy(
            src_ref=source,
            dst_ref=target,
            send_sem=sems.at[0, at_send],
            recv_sem=sems.at[1, at_recv],
            device_id=device,
            device_id_type=pl.DeviceIdType.MESH,
        )
        copy.start()
        started.append(copy)

    def to_plane(ref, sems):
        for c in cols:
            push(ref.at[my_c], ref.at[my_c], sems, c, my_c, (my_r, c))

    def to_line(source, ref, sems):
        for r in rows:
            at = my_r if source is None else r
            push((ref if source is None else source).at[at], ref.at[my_r], sems, r, my_r, (r, my_c))

    def arrived(ref, sems, at):
        pltpu.make_async_remote_copy(
            src_ref=ref.at[at],
            dst_ref=ref.at[at],
            send_sem=sems.at[0, at],
            recv_sem=sems.at[1, at],
            device_id=(my_r, my_c),
            device_id_type=pl.DeviceIdType.MESH,
        ).wait_recv()

    pad_f[...] = jnp.zeros_like(pad_f)
    pad_i[...] = jnp.zeros_like(pad_i)
    vec_col[my_c] = jnp.zeros((rhs, LANES), jnp.float32)
    for load in loads:
        load.wait()
    pad_f[0:3, 0:width] = vertices_ref[...]
    pad_i[0:4, 0:width] = connect_ref[...]
    pad_i[4:5, 0:width] = component_ref[...]
    vec_col[my_c, :, 0:width] = rhs_ref[...]
    vertices = pad_f[...]
    corners = [
        jnp.take_along_axis(
            vertices,
            jnp.broadcast_to(pad_i[k : k + 1, :], vertices.shape),
            axis=1,
            mode="promise_in_bounds",
        )
        for k in range(4)
    ]
    center, area = panel_frame(corners, pad_i[4:5, :], azimuth_ref[0], BLADES)
    size = jnp.sqrt(area[0] * area[0] + area[1] * area[1] + area[2] * area[2])
    frame = jnp.concatenate(
        center + [scale * part for part in area] + [jnp.zeros((2, LANES), jnp.float32)], axis=0
    )
    frames_col[my_c] = frame
    frames_row[my_r] = frame

    pl.semaphore_wait(barrier, nc - 1 + nr - 1)
    to_line(None, frames_row, sems_fr)
    to_plane(frames_col, sems_fc)
    to_plane(vec_col, sems_g)

    def fill(c):
        columns = frames_col[c].T
        for s in range(LANES // SUB):
            x, y, z = (
                jnp.broadcast_to(columns[s * SUB : (s + 1) * SUB, k : k + 1], (SUB, LANES))
                for k in range(3)
            )
            place = pl.ds(pl.multiple_of(c * LANES + s * SUB, SUB), SUB)

            def one(r, carry):
                source = frames_row[r]
                dx, dy, dz = x - source[0:1], y - source[1:2], z - source[2:3]
                inverse = lax.rsqrt(dx * dx + dy * dy + (dz * dz + core_square))
                along = source[3:4] * dx + source[4:5] * dy + source[5:6] * dz
                value = inverse * (along * (inverse * inverse) + source[5:6])
                lead = value.astype(jnp.bfloat16)
                where = pl.ds(r * LANES if isinstance(r, int) else pl.multiple_of(r * LANES, LANES), LANES)
                matrix[0, place, where] = lead
                matrix[1, place, where] = (value - lead.astype(jnp.float32)).astype(jnp.bfloat16)
                return carry

            if nr <= 4:
                for r in range(nr):
                    one(r, 0)
            else:
                lax.fori_loop(0, nr, one, 0)

    def fill_step(k, carry):
        c = lax.rem(my_c + k, nc)
        arrived(frames_col, sems_fc, c)
        fill(c)
        return carry

    for r in rows:
        arrived(frames_row, sems_fr, r)
    fill(my_c)
    lax.fori_loop(1, nc, fill_step, 0)

    def place_halves(ref, c):
        halves[:, pl.ds(pl.multiple_of(c * LANES, LANES), LANES)] = split(ref[c])

    def product(ref, sems):
        def chip(k, total):
            first = lax.rem(my_c // 2 + k, nc // 2) * 2
            for c in (first, first + 1):

                @pl.when(c != my_c)
                def _():
                    arrived(ref, sems, c)

                place_halves(ref, c)
            at = pl.ds(pl.multiple_of(first * LANES, 2 * LANES), 2 * LANES)
            part = jnp.dot(
                halves[:, at], matrix[0, at, :], preferred_element_type=jnp.float32
            ) + jnp.dot(halves[:, at], matrix[1, at, :], preferred_element_type=jnp.float32)
            return part if total is None else total + part

        total = chip(0, None)
        if nc <= 8:
            for k in range(1, nc // 2):
                total = chip(k, total)
        else:
            total = lax.fori_loop(1, nc // 2, chip, total)
        return total[:rhs] + total[rhs:]

    def apply_matrix(ref, sems_ref, send, recv, sems):
        total = product(ref, sems_ref)
        for r in range(nr):
            send[r] = total[:, r * LANES : (r + 1) * LANES]
        to_line(send, recv, sems)
        summed = send[my_r] + size * ref[my_c]
        for r in rows:
            arrived(recv, sems, r)
            summed = summed + recv[r]
        return summed

    w1 = apply_matrix(vec_col, sems_g, send_one, recv_one, sems_one)
    image_col[my_c] = w1
    to_plane(image_col, sems_w)
    g = vec_col[my_c]
    lane = lax.broadcasted_iota(jnp.int32, (rhs, LANES), 1)

    def with_sum(tile, at, product):
        return jnp.where(lane == at, jnp.sum(product, axis=1, keepdims=True), tile)

    tile = jnp.zeros((rhs, LANES), jnp.float32)
    tile = with_sum(tile, 0, g * g)
    tile = with_sum(tile, 1, g * w1)
    tile = with_sum(tile, 2, w1 * w1)
    w2 = apply_matrix(image_col, sems_w, send_two, recv_two, sems_two)
    tile = with_sum(tile, 3, g * w2)
    tile = with_sum(tile, 4, w1 * w2)
    tile = with_sum(tile, 5, w2 * w2)

    total_col[my_c] = jnp.zeros((8, LANES), jnp.float32)
    total_col[my_c, :, 0:rhs] = tile.T[0:8, :]
    to_plane(total_col, sems_tc)
    for c in cols:
        arrived(total_col, sems_tc, c)
    total = total_col[0]
    for c in range(1, nc):
        total = total + total_col[c]
    total_row[my_r] = total
    to_line(None, total_row, sems_tr)
    for r in rows:
        arrived(total_row, sems_tr, r)
    total = total_row[0]
    for r in range(1, nr):
        total = total + total_row[r]
    of_g, of_w1, residual = small_solve(*(total[k : k + 1] for k in range(6)))
    residual_ref[...] = residual[:, 0:rhs]
    factors = jnp.concatenate([of_g, of_w1, jnp.zeros((6, LANES), jnp.float32)], axis=0).T
    answer = factors[0:rhs, 0:1] * g + factors[0:rhs, 1:2] * w1
    solution_ref[...] = answer[:, 0:width]
    for copy in started:
        copy.wait_send()


def on_device(nr, nc, vertices, connect, component, azimuth, adjoint_rhs):
    rhs, width = adjoint_rhs.shape
    vmem = pl.BlockSpec(memory_space=pltpu.VMEM)
    f32 = jnp.float32
    matrix_bytes = 2 * nc * nr * LANES * LANES * 2
    pair = lambda n: pltpu.SemaphoreType.DMA((2, n))
    answer, residual = pl.pallas_call(
        functools.partial(kernel, nr, nc, width, rhs),
        out_shape=(
            jax.ShapeDtypeStruct((rhs, width), f32),
            jax.ShapeDtypeStruct((1, rhs), f32),
        ),
        in_specs=[pl.BlockSpec(memory_space=pltpu.HBM)] * 5,
        out_specs=(vmem, vmem),
        scratch_shapes=[
            pltpu.SMEM((1,), f32),
            pltpu.VMEM((3, width), f32),
            pltpu.VMEM((4, width), jnp.int32),
            pltpu.VMEM((1, width), jnp.int32),
            pltpu.VMEM((rhs, width), f32),
            pltpu.SemaphoreType.DMA((5,)),
            pltpu.VMEM((8, LANES), f32),
            pltpu.VMEM((8, LANES), jnp.int32),
            pltpu.VMEM((nc, 8, LANES), f32),
            pltpu.VMEM((nr, 8, LANES), f32),
            pltpu.VMEM((nc, rhs, LANES), f32),
            pltpu.VMEM((nc, rhs, LANES), f32),
            pltpu.VMEM((2 * rhs, nc * LANES), jnp.bfloat16),
            pltpu.VMEM((2, nc * LANES, nr * LANES), jnp.bfloat16),
            pltpu.VMEM((nr, rhs, LANES), f32),
            pltpu.VMEM((nr, rhs, LANES), f32),
            pltpu.VMEM((nr, rhs, LANES), f32),
            pltpu.VMEM((nr, rhs, LANES), f32),
            pltpu.VMEM((nc, 8, LANES), f32),
            pltpu.VMEM((nr, 8, LANES), f32),
            pair(nc), pair(nr), pair(nc), pair(nc), pair(nr), pair(nr), pair(nc), pair(nr),
        ],
        compiler_params=pltpu.CompilerParams(
            collective_id=0,
            has_side_effects=True,
            vmem_limit_bytes=64 * 1024 * 1024,
        ),
        cost_estimate=pl.CostEstimate(
            flops=2 * matrix_bytes * rhs, bytes_accessed=4 * rhs * width * 3, transcendentals=0
        ),
    )(azimuth, vertices, connect, component.reshape(1, width), adjoint_rhs)
    return answer, residual.reshape(rhs)


def solution(mesh):
    in_specs = (
        P(None, ("row", "col")),
        P(None, ("row", "col")),
        P(("row", "col")),
        P(),
        P(None, ("row", "col")),
    )
    out_specs = (P(None, ("row", "col")), P())
    return jax.shard_map(
        functools.partial(on_device, mesh.shape["row"], mesh.shape["col"]),
        mesh=mesh,
        in_specs=in_specs,
        out_specs=out_specs,
        check_vma=False,
    )
```

```python
import functools
import math

import jax
import jax.numpy as jnp
from jax import lax
from jax.experimental import pallas as pl
from jax.experimental.pallas import tpu as pltpu
from jax.sharding import PartitionSpec as P

BLADES = 4
LANES = 128
SUB = 32

epsilon = 1e-06
core_square = 0.04
shift = 3.0


def panel_frame(corners, component, azimuth, blades):
    angle_turn = azimuth + 2.0 * math.pi / blades * (component - 1).astype(jnp.float32)
    cosine = jnp.cos(angle_turn)
    sine = jnp.sin(angle_turn)
    on_rotor = component > 0
    placed = []
    for corner in corners:
        x, y, z = corner[0:1], corner[1:2], corner[2:3]
        placed.append(
            (
                jnp.where(on_rotor, cosine * x - sine * y, x),
                jnp.where(on_rotor, sine * x + cosine * y, y),
                z,
            )
        )
    center = [
        (placed[0][k] + placed[1][k] + placed[2][k] + placed[3][k]) * 0.25 for k in range(3)
    ]
    one = [placed[2][k] - placed[0][k] for k in range(3)]
    two = [placed[3][k] - placed[1][k] for k in range(3)]
    area = [
        0.5 * (one[1] * two[2] - one[2] * two[1]),
        0.5 * (one[2] * two[0] - one[0] * two[2]),
        0.5 * (one[0] * two[1] - one[1] * two[0]),
    ]
    return center, area


def small_solve(gg, p1, p2, q0, q1, q2):
    n2 = gg + epsilon
    start_norm = jnp.sqrt(n2)
    one_one = gg / n2
    first_diag = p1 / n2 + shift * one_one
    sigma = (p1 - shift * epsilon) / n2
    uu = jnp.maximum((p2 - 2.0 * sigma * p1 + sigma * sigma * gg) / n2, 0.0)
    sub2 = uu + epsilon
    first_sub = jnp.sqrt(sub2)
    one_two = (p1 + shift * gg) * (epsilon / n2) / (n2 * first_sub)
    t0 = (q0 - sigma * p1) / (n2 * first_sub)
    second_top = t0 + shift * one_two
    two_two = uu / sub2
    t1 = (q1 - sigma * (p2 + q0 - sigma * p1)) / (n2 * sub2)
    second_diag = t1 + shift * two_two
    tau = t1 - shift * epsilon / sub2
    yy = (q2 - sigma * (2.0 * q1 - sigma * p2)) / (n2 * sub2)
    vv = (
        yy
        - 2.0 * (second_top * t0 + tau * t1)
        + second_top * second_top * one_one
        + tau * tau * two_two
        + 2.0 * second_top * tau * one_two
    )
    second_sub = jnp.sqrt(jnp.maximum(vv, 0.0) + epsilon)
    gram_00 = first_diag * first_diag + first_sub * first_sub
    cross = first_diag * second_diag - first_sub * second_top
    det_value = second_sub * second_sub * gram_00 + cross * cross
    gram_01 = first_diag * second_top + first_sub * second_diag
    gram_11 = second_top * second_top + second_diag * second_diag + second_sub * second_sub
    coef_one = start_norm * (gram_11 * first_diag - gram_01 * second_top) / det_value
    coef_two = start_norm * (gram_00 * second_top - gram_01 * first_diag) / det_value
    error_one = start_norm - first_diag * coef_one - second_top * coef_two
    error_two = -first_sub * coef_one - second_diag * coef_two
    error_three = -second_sub * coef_two
    residual = error_one * error_one + error_two * error_two + error_three * error_three
    of_w1 = coef_two / (start_norm * first_sub)
    of_g = coef_one / start_norm - sigma * of_w1
    return of_g, of_w1, residual


def split(value):
    twice = jnp.concatenate([value, value], axis=0)
    lead = twice.astype(jnp.bfloat16).astype(jnp.float32)
    row = lax.broadcasted_iota(jnp.int32, twice.shape, 0)
    return jnp.where(row < value.shape[0], lead, twice - lead).astype(jnp.bfloat16)


def kernel(
    nr, nc, width, rhs,
    azimuth_in, vertices_in, connect_in, component_in, rhs_in,
    solution_ref, residual_ref,
    azimuth_ref, vertices_ref, connect_ref, component_ref, rhs_ref, sems_in,
    pad_f, pad_i, frames_col, frames_row, vec_col, image_col, halves, matrix,
    send_one, recv_one, send_two, recv_two, total_row, total_all,
    sems_fc, sems_fr, sems_g, sems_w, sems_one, sems_two, sems_tr, sems_ta,
):
    my_r, my_c = lax.axis_index("row"), lax.axis_index("col")
    scale = 2.0 / math.sqrt(width * nr * nc)
    cols = [lax.rem(my_c + k, nc) for k in range(1, nc)]
    rows = [lax.rem(my_r + k, nr) for k in range(1, nr)]

    loads = [
        pltpu.make_async_copy(source, target, sems_in.at[k])
        for k, (source, target) in enumerate(
            (
                (azimuth_in, azimuth_ref),
                (vertices_in, vertices_ref),
                (connect_in, connect_ref),
                (component_in, component_ref),
                (rhs_in, rhs_ref),
            )
        )
    ]
    for load in loads:
        load.start()
    barrier = pltpu.get_barrier_semaphore()
    devices = nr * nc
    me = my_r * nc + my_c
    order = sorted(range(1, devices), key=lambda k: abs(k - devices // 2))

    def each_other(act):
        def step(k, carry):
            act(lax.rem(me + k, devices))
            return carry

        if devices <= 64:
            for k in order:
                step(k, 0)
        else:
            lax.fori_loop(1, devices, step, 0)

    def greet(other):
        pl.semaphore_signal(
            barrier,
            inc=1,
            device_id=(other // nc, lax.rem(other, nc)),
            device_id_type=pl.DeviceIdType.MESH,
        )

    each_other(greet)

    started = []

    def push(source, target, sems, at_send, at_recv, device):
        copy = pltpu.make_async_remote_copy(
            src_ref=source,
            dst_ref=target,
            send_sem=sems.at[0, at_send],
            recv_sem=sems.at[1, at_recv],
            device_id=device,
            device_id_type=pl.DeviceIdType.MESH,
        )
        copy.start()
        started.append(copy)

    def to_plane(ref, sems):
        for c in cols:
            push(ref.at[my_c], ref.at[my_c], sems, c, my_c, (my_r, c))

    def to_line(source, ref, sems):
        for r in rows:
            at = my_r if source is None else r
            push((ref if source is None else source).at[at], ref.at[my_r], sems, r, my_r, (r, my_c))

    def arrived(ref, sems, at):
        pltpu.make_async_remote_copy(
            src_ref=ref.at[at],
            dst_ref=ref.at[at],
            send_sem=sems.at[0, at],
            recv_sem=sems.at[1, at],
            device_id=(my_r, my_c),
            device_id_type=pl.DeviceIdType.MESH,
        ).wait_recv()

    pad_f[...] = jnp.zeros_like(pad_f)
    pad_i[...] = jnp.zeros_like(pad_i)
    vec_col[my_c] = jnp.zeros((rhs, LANES), jnp.float32)
    for load in loads:
        load.wait()
    pad_f[0:3, 0:width] = vertices_ref[...]
    pad_i[0:4, 0:width] = connect_ref[...]
    pad_i[4:5, 0:width] = component_ref[...]
    vec_col[my_c, :, 0:width] = rhs_ref[...]
    vertices = pad_f[...]
    corners = [
        jnp.take_along_axis(
            vertices,
            jnp.broadcast_to(pad_i[k : k + 1, :], vertices.shape),
            axis=1,
            mode="promise_in_bounds",
        )
        for k in range(4)
    ]
    center, area = panel_frame(corners, pad_i[4:5, :], azimuth_ref[0], BLADES)
    size = jnp.sqrt(area[0] * area[0] + area[1] * area[1] + area[2] * area[2])
    frame = jnp.concatenate(
        center + [scale * part for part in area] + [jnp.zeros((2, LANES), jnp.float32)], axis=0
    )
    frames_col[my_c] = frame
    frames_row[my_r] = frame

    pl.semaphore_wait(barrier, devices - 1)
    to_line(None, frames_row, sems_fr)
    to_plane(frames_col, sems_fc)
    to_plane(vec_col, sems_g)

    def fill(c):
        columns = frames_col[c].T
        for s in range(LANES // SUB):
            x, y, z = (
                jnp.broadcast_to(columns[s * SUB : (s + 1) * SUB, k : k + 1], (SUB, LANES))
                for k in range(3)
            )
            place = pl.ds(pl.multiple_of(c * LANES + s * SUB, SUB), SUB)

            def one(r, carry):
                source = frames_row[r]
                dx, dy, dz = x - source[0:1], y - source[1:2], z - source[2:3]
                inverse = lax.rsqrt(dx * dx + dy * dy + (dz * dz + core_square))
                along = source[3:4] * dx + source[4:5] * dy + source[5:6] * dz
                value = inverse * (along * (inverse * inverse) + source[5:6])
                lead = value.astype(jnp.bfloat16)
                where = pl.ds(r * LANES if isinstance(r, int) else pl.multiple_of(r * LANES, LANES), LANES)
                matrix[0, place, where] = lead
                matrix[1, place, where] = (value - lead.astype(jnp.float32)).astype(jnp.bfloat16)
                return carry

            if nr <= 4:
                for r in range(nr):
                    one(r, 0)
            else:
                lax.fori_loop(0, nr, one, 0)

    def fill_step(k, carry):
        c = lax.rem(my_c + k, nc)
        arrived(frames_col, sems_fc, c)
        fill(c)
        return carry

    for r in rows:
        arrived(frames_row, sems_fr, r)
    fill(my_c)
    lax.fori_loop(1, nc, fill_step, 0)

    def place_halves(ref, c):
        halves[:, pl.ds(pl.multiple_of(c * LANES, LANES), LANES)] = split(ref[c])

    def product(ref, sems):
        def chip(k, total):
            first = lax.rem(my_c // 2 + k, nc // 2) * 2
            for c in (first, first + 1):

                @pl.when(c != my_c)
                def _():
                    arrived(ref, sems, c)

                place_halves(ref, c)
            at = pl.ds(pl.multiple_of(first * LANES, 2 * LANES), 2 * LANES)
            part = jnp.dot(
                halves[:, at], matrix[0, at, :], preferred_element_type=jnp.float32
            ) + jnp.dot(halves[:, at], matrix[1, at, :], preferred_element_type=jnp.float32)
            return part if total is None else total + part

        total = chip(0, None)
        if nc <= 8:
            for k in range(1, nc // 2):
                total = chip(k, total)
        else:
            total = lax.fori_loop(1, nc // 2, chip, total)
        return total[:rhs] + total[rhs:]

    def apply_matrix(ref, sems_ref, send, recv, sems, beside=None):
        total = product(ref, sems_ref)
        for r in range(nr):
            send[r] = total[:, r * LANES : (r + 1) * LANES]
        to_line(send, recv, sems)
        if beside is not None:
            beside()
        summed = send[my_r] + size * ref[my_c]
        for r in rows:
            arrived(recv, sems, r)
            summed = summed + recv[r]
        return summed

    w1 = apply_matrix(vec_col, sems_g, send_one, recv_one, sems_one)
    image_col[my_c] = w1
    to_plane(image_col, sems_w)
    g = vec_col[my_c]
    stride = LANES // 4
    across = lax.broadcasted_iota(jnp.int32, (rhs, LANES), 1) - lax.broadcasted_iota(
        jnp.int32, (rhs, LANES), 0
    )

    def as_row(products):
        tile = jnp.zeros((rhs, LANES), jnp.float32)
        for k, values in enumerate(products):
            tile = jnp.where(
                across == k * stride, jnp.sum(values, axis=1, keepdims=True), tile
            )
        return jnp.sum(tile, axis=0, keepdims=True)

    def fields(row):
        return [row[:, k * stride : k * stride + rhs] for k in range(3)]

    def plane_sums():
        def add(c, sums):
            u, v = vec_col[c], image_col[c]
            return sums[0] + u * u, sums[1] + u * v, sums[2] + v * v

        sums = (jnp.zeros((rhs, LANES), jnp.float32),) * 3
        if nc <= 8:
            for c in range(nc):
                sums = add(c, sums)
        else:
            sums = lax.fori_loop(0, nc, add, sums)
        total_row[my_r] = as_row(sums)
        to_line(None, total_row, sems_tr)

    w2 = apply_matrix(image_col, sems_w, send_two, recv_two, sems_two, plane_sums)

    total_all[me] = as_row((g * w2, w1 * w2, w2 * w2))

    def last(other):
        return pltpu.make_async_remote_copy(
            src_ref=total_all.at[me],
            dst_ref=total_all.at[me],
            send_sem=sems_ta.at[0, other],
            recv_sem=sems_ta.at[1, me],
            device_id=(other // nc, lax.rem(other, nc)),
            device_id_type=pl.DeviceIdType.MESH,
        )

    each_other(lambda other: last(other).start())
    for r in rows:
        arrived(total_row, sems_tr, r)
    early = total_row[0]
    for r in range(1, nr):
        early = early + total_row[r]
    each_other(lambda other: arrived(total_all, sems_ta, other))
    if devices <= 64:
        parts = [total_all[k] for k in range(devices)]
        while len(parts) > 1:
            parts = [sum(parts[k : k + 2][1:], parts[k]) for k in range(0, len(parts), 2)]
        late = parts[0]
    else:
        late = lax.fori_loop(1, devices, lambda k, t: t + total_all[k], total_all[0])
    of_g, of_w1, residual = small_solve(*fields(early), *fields(late))
    residual_ref[...] = residual
    pad_f[0:1, 0:rhs] = of_g
    pad_f[1:2, 0:rhs] = of_w1
    factors = pad_f[...].T
    answer = factors[0:rhs, 0:1] * g + factors[0:rhs, 1:2] * w1
    solution_ref[...] = answer[:, 0:width]
    for copy in started:
        copy.wait_send()
    each_other(lambda other: last(other).wait_send())


def on_device(nr, nc, vertices, connect, component, azimuth, adjoint_rhs):
    rhs, width = adjoint_rhs.shape
    vmem = pl.BlockSpec(memory_space=pltpu.VMEM)
    f32 = jnp.float32
    matrix_bytes = 2 * nc * nr * LANES * LANES * 2
    pair = lambda n: pltpu.SemaphoreType.DMA((2, n))
    answer, residual = pl.pallas_call(
        functools.partial(kernel, nr, nc, width, rhs),
        out_shape=(
            jax.ShapeDtypeStruct((rhs, width), f32),
            jax.ShapeDtypeStruct((1, rhs), f32),
        ),
        in_specs=[pl.BlockSpec(memory_space=pltpu.HBM)] * 5,
        out_specs=(vmem, vmem),
        scratch_shapes=[
            pltpu.SMEM((1,), f32),
            pltpu.VMEM((3, width), f32),
            pltpu.VMEM((4, width), jnp.int32),
            pltpu.VMEM((1, width), jnp.int32),
            pltpu.VMEM((rhs, width), f32),
            pltpu.SemaphoreType.DMA((5,)),
            pltpu.VMEM((8, LANES), f32),
            pltpu.VMEM((8, LANES), jnp.int32),
            pltpu.VMEM((nc, 8, LANES), f32),
            pltpu.VMEM((nr, 8, LANES), f32),
            pltpu.VMEM((nc, rhs, LANES), f32),
            pltpu.VMEM((nc, rhs, LANES), f32),
            pltpu.VMEM((2 * rhs, nc * LANES), jnp.bfloat16),
            pltpu.VMEM((2, nc * LANES, nr * LANES), jnp.bfloat16),
            pltpu.VMEM((nr, rhs, LANES), f32),
            pltpu.VMEM((nr, rhs, LANES), f32),
            pltpu.VMEM((nr, rhs, LANES), f32),
            pltpu.VMEM((nr, rhs, LANES), f32),
            pltpu.VMEM((nr, 1, LANES), f32),
            pltpu.VMEM((nr * nc, 1, LANES), f32),
            pair(nc), pair(nr), pair(nc), pair(nc), pair(nr), pair(nr), pair(nr), pair(nr * nc),
        ],
        compiler_params=pltpu.CompilerParams(
            collective_id=0,
            has_side_effects=True,
            vmem_limit_bytes=matrix_bytes + 20 * 1024 * 1024,
        ),
        cost_estimate=pl.CostEstimate(
            flops=2 * matrix_bytes * rhs, bytes_accessed=4 * rhs * width * 3, transcendentals=0
        ),
    )(azimuth, *(pltpu.with_memory_space_constraint(x, pltpu.HBM) for x in (vertices, connect, component.reshape(1, width), adjoint_rhs)))
    return answer, residual.reshape(rhs)


def solution(mesh):
    in_specs = (
        P(None, ("row", "col")),
        P(None, ("row", "col")),
        P(("row", "col")),
        P(),
        P(None, ("row", "col")),
    )
    out_specs = (P(None, ("row", "col")), P())
    return jax.shard_map(
        functools.partial(on_device, mesh.shape["row"], mesh.shape["col"]),
        mesh=mesh,
        in_specs=in_specs,
        out_specs=out_specs,
        check_vma=False,
    )
```

```python
import functools
import math

import jax
import jax.numpy as jnp
from jax import lax
from jax.experimental import pallas as pl
from jax.experimental.pallas import tpu as pltpu
from jax.sharding import PartitionSpec as P

BLADES = 4
LANES = 128
SUB = 32

epsilon = 1e-06
core_square = 0.04
shift = 3.0


def panel_frame(corners, component, azimuth, blades):
    angle_turn = azimuth + 2.0 * math.pi / blades * (component - 1).astype(jnp.float32)
    cosine = jnp.cos(angle_turn)
    sine = jnp.sin(angle_turn)
    on_rotor = component > 0
    placed = []
    for corner in corners:
        x, y, z = corner[0:1], corner[1:2], corner[2:3]
        placed.append(
            (
                jnp.where(on_rotor, cosine * x - sine * y, x),
                jnp.where(on_rotor, sine * x + cosine * y, y),
                z,
            )
        )
    center = [
        (placed[0][k] + placed[1][k] + placed[2][k] + placed[3][k]) * 0.25 for k in range(3)
    ]
    one = [placed[2][k] - placed[0][k] for k in range(3)]
    two = [placed[3][k] - placed[1][k] for k in range(3)]
    area = [
        0.5 * (one[1] * two[2] - one[2] * two[1]),
        0.5 * (one[2] * two[0] - one[0] * two[2]),
        0.5 * (one[0] * two[1] - one[1] * two[0]),
    ]
    return center, area


def small_solve(gg, p1, p2, q0, q1, q2):
    n2 = gg + epsilon
    start_norm = jnp.sqrt(n2)
    one_one = gg / n2
    first_diag = p1 / n2 + shift * one_one
    sigma = (p1 - shift * epsilon) / n2
    uu = jnp.maximum((p2 - 2.0 * sigma * p1 + sigma * sigma * gg) / n2, 0.0)
    sub2 = uu + epsilon
    first_sub = jnp.sqrt(sub2)
    one_two = (p1 + shift * gg) * (epsilon / n2) / (n2 * first_sub)
    t0 = (q0 - sigma * p1) / (n2 * first_sub)
    second_top = t0 + shift * one_two
    two_two = uu / sub2
    t1 = (q1 - sigma * (p2 + q0 - sigma * p1)) / (n2 * sub2)
    second_diag = t1 + shift * two_two
    tau = t1 - shift * epsilon / sub2
    yy = (q2 - sigma * (2.0 * q1 - sigma * p2)) / (n2 * sub2)
    vv = (
        yy
        - 2.0 * (second_top * t0 + tau * t1)
        + second_top * second_top * one_one
        + tau * tau * two_two
        + 2.0 * second_top * tau * one_two
    )
    second_sub = jnp.sqrt(jnp.maximum(vv, 0.0) + epsilon)
    gram_00 = first_diag * first_diag + first_sub * first_sub
    cross = first_diag * second_diag - first_sub * second_top
    det_value = second_sub * second_sub * gram_00 + cross * cross
    gram_01 = first_diag * second_top + first_sub * second_diag
    gram_11 = second_top * second_top + second_diag * second_diag + second_sub * second_sub
    coef_one = start_norm * (gram_11 * first_diag - gram_01 * second_top) / det_value
    coef_two = start_norm * (gram_00 * second_top - gram_01 * first_diag) / det_value
    error_one = start_norm - first_diag * coef_one - second_top * coef_two
    error_two = -first_sub * coef_one - second_diag * coef_two
    error_three = -second_sub * coef_two
    residual = error_one * error_one + error_two * error_two + error_three * error_three
    of_w1 = coef_two / (start_norm * first_sub)
    of_g = coef_one / start_norm - sigma * of_w1
    return of_g, of_w1, residual


def split(value):
    twice = jnp.concatenate([value, value], axis=0)
    lead = twice.astype(jnp.bfloat16).astype(jnp.float32)
    row = lax.broadcasted_iota(jnp.int32, twice.shape, 0)
    return jnp.where(row < value.shape[0], lead, twice - lead).astype(jnp.bfloat16)


def kernel(
    nr, nc, width, rhs,
    azimuth_in, vertices_in, connect_in, component_in, rhs_in,
    solution_ref, residual_ref,
    azimuth_ref, vertices_ref, connect_ref, component_ref, rhs_ref, sems_in,
    pad_f, pad_i, frames_col, frames_row, vec_col, image_col, halves, matrix,
    send_one, recv_one, send_two, recv_two, total_row, total_col, total_end,
    sems_fc, sems_fr, sems_g, sems_w, sems_one, sems_two, sems_tr, sems_tc, sems_te,
):
    my_r, my_c = lax.axis_index("row"), lax.axis_index("col")
    scale = 2.0 / math.sqrt(width * nr * nc)

    def each_col(act):
        lax.fori_loop(1, nc, lambda k, carry: (act(lax.rem(my_c + k, nc)), carry)[1], 0)

    def each_row(act):
        lax.fori_loop(1, nr, lambda k, carry: (act(lax.rem(my_r + k, nr)), carry)[1], 0)

    loads = [
        pltpu.make_async_copy(source, target, sems_in.at[k])
        for k, (source, target) in enumerate(
            (
                (azimuth_in, azimuth_ref),
                (vertices_in, vertices_ref),
                (connect_in, connect_ref),
                (component_in, component_ref),
                (rhs_in, rhs_ref),
            )
        )
    ]
    for load in loads:
        load.start()
    barrier = pltpu.get_barrier_semaphore()

    def greet(device):
        pl.semaphore_signal(
            barrier, inc=1, device_id=device, device_id_type=pl.DeviceIdType.MESH
        )

    each_col(lambda c: greet((my_r, c)))
    each_row(lambda r: greet((r, my_c)))

    started = []

    def push(each, source, target, sems, at_recv, device):
        def copy(other):
            return pltpu.make_async_remote_copy(
                src_ref=source(other),
                dst_ref=target,
                send_sem=sems.at[0, other],
                recv_sem=sems.at[1, at_recv],
                device_id=device(other),
                device_id_type=pl.DeviceIdType.MESH,
            )

        each(lambda other: copy(other).start())
        started.append((each, lambda other: copy(other).wait_send()))

    def to_plane(ref, sems):
        push(each_col, lambda c: ref.at[my_c], ref.at[my_c], sems, my_c, lambda c: (my_r, c))

    def to_line(source, ref, sems):
        pick = (lambda r: ref.at[my_r]) if source is None else (lambda r: source.at[r])
        push(each_row, pick, ref.at[my_r], sems, my_r, lambda r: (r, my_c))

    def arrived(ref, sems, at):
        pltpu.make_async_remote_copy(
            src_ref=ref.at[at],
            dst_ref=ref.at[at],
            send_sem=sems.at[0, at],
            recv_sem=sems.at[1, at],
            device_id=(my_r, my_c),
            device_id_type=pl.DeviceIdType.MESH,
        ).wait_recv()

    pad_f[...] = jnp.zeros_like(pad_f)
    pad_i[...] = jnp.zeros_like(pad_i)
    vec_col[my_c] = jnp.zeros((rhs, LANES), jnp.float32)
    for load in loads:
        load.wait()
    pad_f[0:3, 0:width] = vertices_ref[...]
    pad_i[0:4, 0:width] = connect_ref[...]
    pad_i[4:5, 0:width] = component_ref[...]
    vec_col[my_c, :, 0:width] = rhs_ref[...]
    vertices = pad_f[...]
    corners = [
        jnp.take_along_axis(
            vertices,
            jnp.broadcast_to(pad_i[k : k + 1, :], vertices.shape),
            axis=1,
            mode="promise_in_bounds",
        )
        for k in range(4)
    ]
    center, area = panel_frame(corners, pad_i[4:5, :], azimuth_ref[0], BLADES)
    size = jnp.sqrt(area[0] * area[0] + area[1] * area[1] + area[2] * area[2])
    frame = jnp.concatenate(
        center + [scale * part for part in area] + [jnp.zeros((2, LANES), jnp.float32)], axis=0
    )
    frames_col[my_c] = frame
    frames_row[my_r] = frame

    pl.semaphore_wait(barrier, nc - 1 + nr - 1)
    to_line(None, frames_row, sems_fr)
    to_plane(frames_col, sems_fc)
    to_plane(vec_col, sems_g)

    def fill(c):
        columns = frames_col[c].T
        for s in range(LANES // SUB):
            x, y, z = (
                jnp.broadcast_to(columns[s * SUB : (s + 1) * SUB, k : k + 1], (SUB, LANES))
                for k in range(3)
            )
            place = pl.ds(pl.multiple_of(c * LANES + s * SUB, SUB), SUB)

            def one(r, carry):
                source = frames_row[r]
                dx, dy, dz = x - source[0:1], y - source[1:2], z - source[2:3]
                inverse = lax.rsqrt(dx * dx + dy * dy + (dz * dz + core_square))
                along = source[3:4] * dx + source[4:5] * dy + source[5:6] * dz
                value = inverse * (along * (inverse * inverse) + source[5:6])
                lead = value.astype(jnp.bfloat16)
                where = pl.ds(r * LANES if isinstance(r, int) else pl.multiple_of(r * LANES, LANES), LANES)
                matrix[0, place, where] = lead
                matrix[1, place, where] = (value - lead.astype(jnp.float32)).astype(jnp.bfloat16)
                return carry

            if nr <= 4:
                for r in range(nr):
                    one(r, 0)
            else:
                lax.fori_loop(0, nr, one, 0)

    def fill_step(k, carry):
        c = lax.rem(my_c + k, nc)

        @pl.when(k > 0)
        def _():
            arrived(frames_col, sems_fc, c)

        fill(c)
        return carry

    each_row(lambda r: arrived(frames_row, sems_fr, r))
    lax.fori_loop(0, nc, fill_step, 0)

    def place_halves(ref, c):
        halves[:, pl.ds(pl.multiple_of(c * LANES, LANES), LANES)] = split(ref[c])

    def product(ref, sems):
        def chip(k, total):
            first = lax.rem(my_c // 2 + k, nc // 2) * 2
            for c in (first, first + 1):

                @pl.when(c != my_c)
                def _():
                    arrived(ref, sems, c)

                place_halves(ref, c)
            at = pl.ds(pl.multiple_of(first * LANES, 2 * LANES), 2 * LANES)
            part = jnp.dot(
                halves[:, at], matrix[0, at, :], preferred_element_type=jnp.float32
            ) + jnp.dot(halves[:, at], matrix[1, at, :], preferred_element_type=jnp.float32)
            return total + part

        total = jnp.zeros((2 * rhs, nr * LANES), jnp.float32)
        total = lax.fori_loop(0, nc // 2, chip, total)
        return total[:rhs] + total[rhs:]

    def apply_matrix(ref, sems_ref, send, recv, sems, beside=None):
        total = product(ref, sems_ref)
        for r in range(nr):
            send[r] = total[:, r * LANES : (r + 1) * LANES]
        to_line(send, recv, sems)
        recv[my_r] = send[my_r]
        if beside is not None:
            beside()
        each_row(lambda r: arrived(recv, sems, r))
        return size * ref[my_c] + jnp.sum(recv[...], axis=0)

    w1 = apply_matrix(vec_col, sems_g, send_one, recv_one, sems_one)
    image_col[my_c] = w1
    to_plane(image_col, sems_w)
    g = vec_col[my_c]
    stride = LANES // 4
    across = lax.broadcasted_iota(jnp.int32, (rhs, LANES), 1) - lax.broadcasted_iota(
        jnp.int32, (rhs, LANES), 0
    )

    def as_row(products):
        tile = jnp.zeros((rhs, LANES), jnp.float32)
        for k, values in enumerate(products):
            tile = jnp.where(
                across == k * stride, jnp.sum(values, axis=1, keepdims=True), tile
            )
        return jnp.sum(tile, axis=0, keepdims=True)

    def fields(row):
        return [row[:, k * stride : k * stride + rhs] for k in range(3)]

    def plane_sums():
        def add(c, sums):
            u, v = vec_col[c], image_col[c]
            return sums[0] + u * u, sums[1] + u * v, sums[2] + v * v

        sums = (jnp.zeros((rhs, LANES), jnp.float32),) * 3
        total_row[my_r] = as_row(lax.fori_loop(0, nc, add, sums))
        to_line(None, total_row, sems_tr)

    w2 = apply_matrix(image_col, sems_w, send_two, recv_two, sems_two, plane_sums)

    total_col[my_c] = as_row((g * w2, w1 * w2, w2 * w2))
    to_plane(total_col, sems_tc)
    each_row(lambda r: arrived(total_row, sems_tr, r))
    early = jnp.sum(total_row[...], axis=0)
    each_col(lambda c: arrived(total_col, sems_tc, c))
    total_end[my_r] = jnp.sum(total_col[...], axis=0)
    to_line(None, total_end, sems_te)
    each_row(lambda r: arrived(total_end, sems_te, r))
    late = jnp.sum(total_end[...], axis=0)
    of_g, of_w1, residual = small_solve(*fields(early), *fields(late))
    residual_ref[...] = residual
    pad_f[0:1, 0:rhs] = of_g
    pad_f[1:2, 0:rhs] = of_w1
    factors = pad_f[...].T
    answer = factors[0:rhs, 0:1] * g + factors[0:rhs, 1:2] * w1
    solution_ref[...] = answer[:, 0:width]
    for each, finish in started:
        each(finish)


def on_device(nr, nc, vertices, connect, component, azimuth, adjoint_rhs):
    rhs, width = adjoint_rhs.shape
    vmem = pl.BlockSpec(memory_space=pltpu.VMEM)
    f32 = jnp.float32
    matrix_bytes = 2 * nc * nr * LANES * LANES * 2
    pair = lambda n: pltpu.SemaphoreType.DMA((2, n))
    answer, residual = pl.pallas_call(
        functools.partial(kernel, nr, nc, width, rhs),
        out_shape=(
            jax.ShapeDtypeStruct((rhs, width), f32),
            jax.ShapeDtypeStruct((1, rhs), f32),
        ),
        in_specs=[pl.BlockSpec(memory_space=pltpu.HBM)] * 5,
        out_specs=(vmem, vmem),
        scratch_shapes=[
            pltpu.SMEM((1,), f32),
            pltpu.VMEM((3, width), f32),
            pltpu.VMEM((4, width), jnp.int32),
            pltpu.VMEM((1, width), jnp.int32),
            pltpu.VMEM((rhs, width), f32),
            pltpu.SemaphoreType.DMA((5,)),
            pltpu.VMEM((8, LANES), f32),
            pltpu.VMEM((8, LANES), jnp.int32),
            pltpu.VMEM((nc, 8, LANES), f32),
            pltpu.VMEM((nr, 8, LANES), f32),
            pltpu.VMEM((nc, rhs, LANES), f32),
            pltpu.VMEM((nc, rhs, LANES), f32),
            pltpu.VMEM((2 * rhs, nc * LANES), jnp.bfloat16),
            pltpu.VMEM((2, nc * LANES, nr * LANES), jnp.bfloat16),
            pltpu.VMEM((nr, rhs, LANES), f32),
            pltpu.VMEM((nr, rhs, LANES), f32),
            pltpu.VMEM((nr, rhs, LANES), f32),
            pltpu.VMEM((nr, rhs, LANES), f32),
            pltpu.VMEM((nr, 1, LANES), f32),
            pltpu.VMEM((nc, 1, LANES), f32),
            pltpu.VMEM((nr, 1, LANES), f32),
            pair(nc), pair(nr), pair(nc), pair(nc), pair(nr), pair(nr), pair(nr), pair(nc), pair(nr),
        ],
        compiler_params=pltpu.CompilerParams(
            collective_id=0,
            has_side_effects=True,
            vmem_limit_bytes=matrix_bytes + 20 * 1024 * 1024,
        ),
        cost_estimate=pl.CostEstimate(
            flops=2 * matrix_bytes * rhs, bytes_accessed=4 * rhs * width * 3, transcendentals=0
        ),
    )(azimuth, *(pltpu.with_memory_space_constraint(x, pltpu.HBM) for x in (vertices, connect, component.reshape(1, width), adjoint_rhs)))
    return answer, residual.reshape(rhs)


def solution(mesh):
    in_specs = (
        P(None, ("row", "col")),
        P(None, ("row", "col")),
        P(("row", "col")),
        P(),
        P(None, ("row", "col")),
    )
    out_specs = (P(None, ("row", "col")), P())
    return jax.shard_map(
        functools.partial(on_device, mesh.shape["row"], mesh.shape["col"]),
        mesh=mesh,
        in_specs=in_specs,
        out_specs=out_specs,
        check_vma=False,
    )
```

```python
import functools
import math

import jax
import jax.numpy as jnp
from jax import lax
from jax.experimental import pallas as pl
from jax.experimental.pallas import tpu as pltpu
from jax.sharding import PartitionSpec as P

BLADES = 4
LANES = 128
SUB = 32

epsilon = 1e-06
core_square = 0.04
shift = 3.0


def panel_frame(corners, component, azimuth, blades):
    angle_turn = azimuth + 2.0 * math.pi / blades * (component - 1).astype(jnp.float32)
    cosine = jnp.cos(angle_turn)
    sine = jnp.sin(angle_turn)
    on_rotor = component > 0
    placed = []
    for corner in corners:
        x, y, z = corner[0:1], corner[1:2], corner[2:3]
        placed.append(
            (
                jnp.where(on_rotor, cosine * x - sine * y, x),
                jnp.where(on_rotor, sine * x + cosine * y, y),
                z,
            )
        )
    center = [
        (placed[0][k] + placed[1][k] + placed[2][k] + placed[3][k]) * 0.25 for k in range(3)
    ]
    one = [placed[2][k] - placed[0][k] for k in range(3)]
    two = [placed[3][k] - placed[1][k] for k in range(3)]
    area = [
        0.5 * (one[1] * two[2] - one[2] * two[1]),
        0.5 * (one[2] * two[0] - one[0] * two[2]),
        0.5 * (one[0] * two[1] - one[1] * two[0]),
    ]
    return center, area


def small_solve(gg, p1, p2, q0, q1, q2):
    n2 = gg + epsilon
    start_norm = jnp.sqrt(n2)
    one_one = gg / n2
    first_diag = p1 / n2 + shift * one_one
    sigma = (p1 - shift * epsilon) / n2
    uu = jnp.maximum((p2 - 2.0 * sigma * p1 + sigma * sigma * gg) / n2, 0.0)
    sub2 = uu + epsilon
    first_sub = jnp.sqrt(sub2)
    one_two = (p1 + shift * gg) * (epsilon / n2) / (n2 * first_sub)
    t0 = (q0 - sigma * p1) / (n2 * first_sub)
    second_top = t0 + shift * one_two
    two_two = uu / sub2
    t1 = (q1 - sigma * (p2 + q0 - sigma * p1)) / (n2 * sub2)
    second_diag = t1 + shift * two_two
    tau = t1 - shift * epsilon / sub2
    yy = (q2 - sigma * (2.0 * q1 - sigma * p2)) / (n2 * sub2)
    vv = (
        yy
        - 2.0 * (second_top * t0 + tau * t1)
        + second_top * second_top * one_one
        + tau * tau * two_two
        + 2.0 * second_top * tau * one_two
    )
    second_sub = jnp.sqrt(jnp.maximum(vv, 0.0) + epsilon)
    gram_00 = first_diag * first_diag + first_sub * first_sub
    cross = first_diag * second_diag - first_sub * second_top
    det_value = second_sub * second_sub * gram_00 + cross * cross
    gram_01 = first_diag * second_top + first_sub * second_diag
    gram_11 = second_top * second_top + second_diag * second_diag + second_sub * second_sub
    coef_one = start_norm * (gram_11 * first_diag - gram_01 * second_top) / det_value
    coef_two = start_norm * (gram_00 * second_top - gram_01 * first_diag) / det_value
    error_one = start_norm - first_diag * coef_one - second_top * coef_two
    error_two = -first_sub * coef_one - second_diag * coef_two
    error_three = -second_sub * coef_two
    residual = error_one * error_one + error_two * error_two + error_three * error_three
    of_w1 = coef_two / (start_norm * first_sub)
    of_g = coef_one / start_norm - sigma * of_w1
    return of_g, of_w1, residual


def split(value):
    twice = jnp.concatenate([value, value], axis=0)
    lead = twice.astype(jnp.bfloat16).astype(jnp.float32)
    row = lax.broadcasted_iota(jnp.int32, twice.shape, 0)
    return jnp.where(row < value.shape[0], lead, twice - lead).astype(jnp.bfloat16)


def kernel(
    nr, nc, width, rhs,
    azimuth_in, vertices_in, connect_in, component_in, rhs_in,
    solution_ref, residual_ref,
    azimuth_ref, vertices_ref, connect_ref, component_ref, rhs_ref, sems_in,
    pad_f, pad_i, frames_col, frames_row, vec_col, image_col, halves, matrix,
    send_one, recv_one, send_two, recv_two, total_row, total_col, total_end,
    sems_fc, sems_fr, sems_g, sems_w, sems_one, sems_two, sems_tr, sems_tc, sems_te,
):
    my_r, my_c = lax.axis_index("row"), lax.axis_index("col")
    scale = 2.0 / math.sqrt(width * nr * nc)

    def loop(start, stop, step, carry):
        if stop <= 8:
            for k in range(start, stop):
                carry = step(k, carry)
            return carry
        return lax.fori_loop(start, stop, step, carry)

    def each_col(act):
        loop(1, nc, lambda k, carry: (act(lax.rem(my_c + k, nc)), carry)[1], 0)

    def each_row(act):
        loop(1, nr, lambda k, carry: (act(lax.rem(my_r + k, nr)), carry)[1], 0)

    loads = [
        pltpu.make_async_copy(source, target, sems_in.at[k])
        for k, (source, target) in enumerate(
            (
                (azimuth_in, azimuth_ref),
                (vertices_in, vertices_ref),
                (connect_in, connect_ref),
                (component_in, component_ref),
                (rhs_in, rhs_ref),
            )
        )
    ]
    for load in loads:
        load.start()
    barrier = pltpu.get_barrier_semaphore()

    def greet(device):
        pl.semaphore_signal(
            barrier, inc=1, device_id=device, device_id_type=pl.DeviceIdType.MESH
        )

    each_col(lambda c: greet((my_r, c)))
    each_row(lambda r: greet((r, my_c)))

    started = []

    def push(each, source, target, sems, at_recv, device):
        def copy(other):
            return pltpu.make_async_remote_copy(
                src_ref=source(other),
                dst_ref=target,
                send_sem=sems.at[0, other],
                recv_sem=sems.at[1, at_recv],
                device_id=device(other),
                device_id_type=pl.DeviceIdType.MESH,
            )

        each(lambda other: copy(other).start())
        started.append((each, lambda other: copy(other).wait_send()))

    def to_plane(ref, sems):
        push(each_col, lambda c: ref.at[my_c], ref.at[my_c], sems, my_c, lambda c: (my_r, c))

    def to_line(source, ref, sems):
        pick = (lambda r: ref.at[my_r]) if source is None else (lambda r: source.at[r])
        push(each_row, pick, ref.at[my_r], sems, my_r, lambda r: (r, my_c))

    def arrived(ref, sems, at):
        pltpu.make_async_remote_copy(
            src_ref=ref.at[at],
            dst_ref=ref.at[at],
            send_sem=sems.at[0, at],
            recv_sem=sems.at[1, at],
            device_id=(my_r, my_c),
            device_id_type=pl.DeviceIdType.MESH,
        ).wait_recv()

    pad_f[...] = jnp.zeros_like(pad_f)
    pad_i[...] = jnp.zeros_like(pad_i)
    vec_col[my_c] = jnp.zeros((rhs, LANES), jnp.float32)
    for load in loads:
        load.wait()
    pad_f[0:3, 0:width] = vertices_ref[...]
    pad_i[0:4, 0:width] = connect_ref[...]
    pad_i[4:5, 0:width] = component_ref[...]
    vec_col[my_c, :, 0:width] = rhs_ref[...]
    vertices = pad_f[...]
    corners = [
        jnp.take_along_axis(
            vertices,
            jnp.broadcast_to(pad_i[k : k + 1, :], vertices.shape),
            axis=1,
            mode="promise_in_bounds",
        )
        for k in range(4)
    ]
    center, area = panel_frame(corners, pad_i[4:5, :], azimuth_ref[0], BLADES)
    size = jnp.sqrt(area[0] * area[0] + area[1] * area[1] + area[2] * area[2])
    frame = jnp.concatenate(
        center + [scale * part for part in area] + [jnp.zeros((2, LANES), jnp.float32)], axis=0
    )
    frames_col[my_c] = frame
    frames_row[my_r] = frame

    pl.semaphore_wait(barrier, nc - 1 + nr - 1)
    to_line(None, frames_row, sems_fr)
    to_plane(frames_col, sems_fc)
    to_plane(vec_col, sems_g)

    def fill(c):
        columns = frames_col[c].T
        for s in range(LANES // SUB):
            x, y, z = (
                jnp.broadcast_to(columns[s * SUB : (s + 1) * SUB, k : k + 1], (SUB, LANES))
                for k in range(3)
            )
            place = pl.ds(pl.multiple_of(c * LANES + s * SUB, SUB), SUB)

            def one(r, carry):
                source = frames_row[r]
                dx, dy, dz = x - source[0:1], y - source[1:2], z - source[2:3]
                inverse = lax.rsqrt(dx * dx + dy * dy + (dz * dz + core_square))
                along = source[3:4] * dx + source[4:5] * dy + source[5:6] * dz
                value = inverse * (along * (inverse * inverse) + source[5:6])
                lead = value.astype(jnp.bfloat16)
                where = pl.ds(r * LANES if isinstance(r, int) else pl.multiple_of(r * LANES, LANES), LANES)
                matrix[0, place, where] = lead
                matrix[1, place, where] = (value - lead.astype(jnp.float32)).astype(jnp.bfloat16)
                return carry

            if nr <= 4:
                for r in range(nr):
                    one(r, 0)
            else:
                lax.fori_loop(0, nr, one, 0)

    def fill_step(k, carry):
        c = lax.rem(my_c + k, nc)

        @pl.when(k > 0)
        def _():
            arrived(frames_col, sems_fc, c)

        fill(c)
        return carry

    each_row(lambda r: arrived(frames_row, sems_fr, r))
    lax.fori_loop(0, nc, fill_step, 0)

    def place_halves(ref, c):
        halves[:, pl.ds(pl.multiple_of(c * LANES, LANES), LANES)] = split(ref[c])

    def product(ref, sems):
        def chip(k, total):
            first = lax.rem(my_c // 2 + k, nc // 2) * 2
            for c in (first, first + 1):

                @pl.when(c != my_c)
                def _():
                    arrived(ref, sems, c)

                place_halves(ref, c)
            at = pl.ds(pl.multiple_of(first * LANES, 2 * LANES), 2 * LANES)
            part = jnp.dot(
                halves[:, at], matrix[0, at, :], preferred_element_type=jnp.float32
            ) + jnp.dot(halves[:, at], matrix[1, at, :], preferred_element_type=jnp.float32)
            return total + part

        total = jnp.zeros((2 * rhs, nr * LANES), jnp.float32)
        total = loop(0, nc // 2, chip, total)
        return total[:rhs] + total[rhs:]

    def apply_matrix(ref, sems_ref, send, recv, sems, beside=None):
        total = product(ref, sems_ref)
        for r in range(nr):
            send[r] = total[:, r * LANES : (r + 1) * LANES]
        to_line(send, recv, sems)
        recv[my_r] = send[my_r]
        if beside is not None:
            beside()
        each_row(lambda r: arrived(recv, sems, r))
        return size * ref[my_c] + jnp.sum(recv[...], axis=0)

    w1 = apply_matrix(vec_col, sems_g, send_one, recv_one, sems_one)
    image_col[my_c] = w1
    to_plane(image_col, sems_w)
    g = vec_col[my_c]
    stride = LANES // 4
    across = lax.broadcasted_iota(jnp.int32, (rhs, LANES), 1) - lax.broadcasted_iota(
        jnp.int32, (rhs, LANES), 0
    )

    def as_row(products):
        tile = jnp.zeros((rhs, LANES), jnp.float32)
        for k, values in enumerate(products):
            tile = jnp.where(
                across == k * stride, jnp.sum(values, axis=1, keepdims=True), tile
            )
        return jnp.sum(tile, axis=0, keepdims=True)

    def fields(row):
        return [row[:, k * stride : k * stride + rhs] for k in range(3)]

    def plane_sums():
        def add(c, sums):
            u, v = vec_col[c], image_col[c]
            return sums[0] + u * u, sums[1] + u * v, sums[2] + v * v

        sums = (jnp.zeros((rhs, LANES), jnp.float32),) * 3
        total_row[my_r] = as_row(loop(0, nc, add, sums))
        to_line(None, total_row, sems_tr)

    w2 = apply_matrix(image_col, sems_w, send_two, recv_two, sems_two, plane_sums)

    total_col[my_c] = as_row((g * w2, w1 * w2, w2 * w2))
    to_plane(total_col, sems_tc)
    each_row(lambda r: arrived(total_row, sems_tr, r))
    early = jnp.sum(total_row[...], axis=0)
    each_col(lambda c: arrived(total_col, sems_tc, c))
    total_end[my_r] = jnp.sum(total_col[...], axis=0)
    to_line(None, total_end, sems_te)
    each_row(lambda r: arrived(total_end, sems_te, r))
    late = jnp.sum(total_end[...], axis=0)
    of_g, of_w1, residual = small_solve(*fields(early), *fields(late))
    residual_ref[...] = residual
    pad_f[0:1, 0:rhs] = of_g
    pad_f[1:2, 0:rhs] = of_w1
    factors = pad_f[...].T
    answer = factors[0:rhs, 0:1] * g + factors[0:rhs, 1:2] * w1
    solution_ref[...] = answer[:, 0:width]
    for each, finish in started:
        each(finish)


def on_device(nr, nc, vertices, connect, component, azimuth, adjoint_rhs):
    rhs, width = adjoint_rhs.shape
    vmem = pl.BlockSpec(memory_space=pltpu.VMEM)
    f32 = jnp.float32
    matrix_bytes = 2 * nc * nr * LANES * LANES * 2
    pair = lambda n: pltpu.SemaphoreType.DMA((2, n))
    answer, residual = pl.pallas_call(
        functools.partial(kernel, nr, nc, width, rhs),
        out_shape=(
            jax.ShapeDtypeStruct((rhs, width), f32),
            jax.ShapeDtypeStruct((1, rhs), f32),
        ),
        in_specs=[pl.BlockSpec(memory_space=pltpu.HBM)] * 5,
        out_specs=(vmem, vmem),
        scratch_shapes=[
            pltpu.SMEM((1,), f32),
            pltpu.VMEM((3, width), f32),
            pltpu.VMEM((4, width), jnp.int32),
            pltpu.VMEM((1, width), jnp.int32),
            pltpu.VMEM((rhs, width), f32),
            pltpu.SemaphoreType.DMA((5,)),
            pltpu.VMEM((8, LANES), f32),
            pltpu.VMEM((8, LANES), jnp.int32),
            pltpu.VMEM((nc, 8, LANES), f32),
            pltpu.VMEM((nr, 8, LANES), f32),
            pltpu.VMEM((nc, rhs, LANES), f32),
            pltpu.VMEM((nc, rhs, LANES), f32),
            pltpu.VMEM((2 * rhs, nc * LANES), jnp.bfloat16),
            pltpu.VMEM((2, nc * LANES, nr * LANES), jnp.bfloat16),
            pltpu.VMEM((nr, rhs, LANES), f32),
            pltpu.VMEM((nr, rhs, LANES), f32),
            pltpu.VMEM((nr, rhs, LANES), f32),
            pltpu.VMEM((nr, rhs, LANES), f32),
            pltpu.VMEM((nr, 1, LANES), f32),
            pltpu.VMEM((nc, 1, LANES), f32),
            pltpu.VMEM((nr, 1, LANES), f32),
            pair(nc), pair(nr), pair(nc), pair(nc), pair(nr), pair(nr), pair(nr), pair(nc), pair(nr),
        ],
        compiler_params=pltpu.CompilerParams(
            collective_id=0,
            has_side_effects=True,
            vmem_limit_bytes=matrix_bytes + 20 * 1024 * 1024,
        ),
        cost_estimate=pl.CostEstimate(
            flops=2 * matrix_bytes * rhs, bytes_accessed=4 * rhs * width * 3, transcendentals=0
        ),
    )(azimuth, *(pltpu.with_memory_space_constraint(x, pltpu.HBM) for x in (vertices, connect, component.reshape(1, width), adjoint_rhs)))
    return answer, residual.reshape(rhs)


def solution(mesh):
    in_specs = (
        P(None, ("row", "col")),
        P(None, ("row", "col")),
        P(("row", "col")),
        P(),
        P(None, ("row", "col")),
    )
    out_specs = (P(None, ("row", "col")), P())
    return jax.shard_map(
        functools.partial(on_device, mesh.shape["row"], mesh.shape["col"]),
        mesh=mesh,
        in_specs=in_specs,
        out_specs=out_specs,
        check_vma=False,
    )
```

```python
import functools
import math

import jax
import jax.numpy as jnp
from jax import lax
from jax.experimental import pallas as pl
from jax.experimental.pallas import tpu as pltpu
from jax.sharding import PartitionSpec as P

BLADES = 4
LANES = 128
SUB = 32

epsilon = 1e-06
core_square = 0.04
shift = 3.0


def panel_frame(corners, component, azimuth, blades):
    angle_turn = azimuth + 2.0 * math.pi / blades * (component - 1).astype(jnp.float32)
    cosine = jnp.cos(angle_turn)
    sine = jnp.sin(angle_turn)
    on_rotor = component > 0
    placed = []
    for corner in corners:
        x, y, z = corner[0:1], corner[1:2], corner[2:3]
        placed.append(
            (
                jnp.where(on_rotor, cosine * x - sine * y, x),
                jnp.where(on_rotor, sine * x + cosine * y, y),
                z,
            )
        )
    center = [
        (placed[0][k] + placed[1][k] + placed[2][k] + placed[3][k]) * 0.25 for k in range(3)
    ]
    one = [placed[2][k] - placed[0][k] for k in range(3)]
    two = [placed[3][k] - placed[1][k] for k in range(3)]
    area = [
        0.5 * (one[1] * two[2] - one[2] * two[1]),
        0.5 * (one[2] * two[0] - one[0] * two[2]),
        0.5 * (one[0] * two[1] - one[1] * two[0]),
    ]
    return center, area


def small_solve(gg, p1, p2, q0, q1, q2):
    n2 = gg + epsilon
    start_norm = jnp.sqrt(n2)
    one_one = gg / n2
    first_diag = p1 / n2 + shift * one_one
    sigma = (p1 - shift * epsilon) / n2
    uu = jnp.maximum((p2 - 2.0 * sigma * p1 + sigma * sigma * gg) / n2, 0.0)
    sub2 = uu + epsilon
    first_sub = jnp.sqrt(sub2)
    one_two = (p1 + shift * gg) * (epsilon / n2) / (n2 * first_sub)
    t0 = (q0 - sigma * p1) / (n2 * first_sub)
    second_top = t0 + shift * one_two
    two_two = uu / sub2
    t1 = (q1 - sigma * (p2 + q0 - sigma * p1)) / (n2 * sub2)
    second_diag = t1 + shift * two_two
    tau = t1 - shift * epsilon / sub2
    yy = (q2 - sigma * (2.0 * q1 - sigma * p2)) / (n2 * sub2)
    vv = (
        yy
        - 2.0 * (second_top * t0 + tau * t1)
        + second_top * second_top * one_one
        + tau * tau * two_two
        + 2.0 * second_top * tau * one_two
    )
    second_sub = jnp.sqrt(jnp.maximum(vv, 0.0) + epsilon)
    gram_00 = first_diag * first_diag + first_sub * first_sub
    cross = first_diag * second_diag - first_sub * second_top
    det_value = second_sub * second_sub * gram_00 + cross * cross
    gram_01 = first_diag * second_top + first_sub * second_diag
    gram_11 = second_top * second_top + second_diag * second_diag + second_sub * second_sub
    coef_one = start_norm * (gram_11 * first_diag - gram_01 * second_top) / det_value
    coef_two = start_norm * (gram_00 * second_top - gram_01 * first_diag) / det_value
    error_one = start_norm - first_diag * coef_one - second_top * coef_two
    error_two = -first_sub * coef_one - second_diag * coef_two
    error_three = -second_sub * coef_two
    residual = error_one * error_one + error_two * error_two + error_three * error_three
    of_w1 = coef_two / (start_norm * first_sub)
    of_g = coef_one / start_norm - sigma * of_w1
    return of_g, of_w1, residual


def split(value):
    twice = jnp.concatenate([value, value], axis=0)
    lead = twice.astype(jnp.bfloat16).astype(jnp.float32)
    row = lax.broadcasted_iota(jnp.int32, twice.shape, 0)
    return jnp.where(row < value.shape[0], lead, twice - lead).astype(jnp.bfloat16)


def kernel(
    nr, nc, width, rhs,
    azimuth_in, vertices_in, connect_in, component_in, rhs_in,
    solution_ref, residual_ref,
    azimuth_ref, vertices_ref, connect_ref, component_ref, rhs_ref, sems_in,
    pad_f, pad_i, frames_col, frames_row, vec_col, image_col, halves, matrix,
    send_one, recv_one, send_two, recv_two, total_row, total_col, total_end,
    sems_fc, sems_fr, sems_g, sems_w, sems_one, sems_two, sems_tr, sems_tc, sems_te,
):
    my_r, my_c = lax.axis_index("row"), lax.axis_index("col")
    scale = 2.0 / math.sqrt(width * nr * nc)

    def loop(start, stop, step, carry):
        if stop <= 8:
            for k in range(start, stop):
                carry = step(k, carry)
            return carry
        return lax.fori_loop(start, stop, step, carry)

    def each_col(act):
        loop(1, nc, lambda k, carry: (act(lax.rem(my_c + k, nc)), carry)[1], 0)

    def each_row(act):
        loop(1, nr, lambda k, carry: (act(lax.rem(my_r + k, nr)), carry)[1], 0)

    loads = [
        pltpu.make_async_copy(source, target, sems_in.at[k])
        for k, (source, target) in enumerate(
            (
                (azimuth_in, azimuth_ref),
                (vertices_in, vertices_ref),
                (connect_in, connect_ref),
                (component_in, component_ref),
                (rhs_in, rhs_ref),
            )
        )
    ]
    for load in loads:
        load.start()
    barrier = pltpu.get_barrier_semaphore()

    def greet(device):
        pl.semaphore_signal(
            barrier, inc=1, device_id=device, device_id_type=pl.DeviceIdType.MESH
        )

    each_col(lambda c: greet((my_r, c)))
    each_row(lambda r: greet((r, my_c)))

    started = []

    def push(each, source, target, sems, at_recv, device):
        def copy(other):
            return pltpu.make_async_remote_copy(
                src_ref=source(other),
                dst_ref=target,
                send_sem=sems.at[0, other],
                recv_sem=sems.at[1, at_recv],
                device_id=device(other),
                device_id_type=pl.DeviceIdType.MESH,
            )

        each(lambda other: copy(other).start())
        started.append((each, lambda other: copy(other).wait_send()))

    def to_plane(ref, sems):
        push(each_col, lambda c: ref.at[my_c], ref.at[my_c], sems, my_c, lambda c: (my_r, c))

    def to_line(source, ref, sems):
        pick = (lambda r: ref.at[my_r]) if source is None else (lambda r: source.at[r])
        push(each_row, pick, ref.at[my_r], sems, my_r, lambda r: (r, my_c))

    def arrived(ref, sems, at):
        pltpu.make_async_remote_copy(
            src_ref=ref.at[at],
            dst_ref=ref.at[at],
            send_sem=sems.at[0, at],
            recv_sem=sems.at[1, at],
            device_id=(my_r, my_c),
            device_id_type=pl.DeviceIdType.MESH,
        ).wait_recv()

    pad_f[...] = jnp.zeros_like(pad_f)
    pad_i[...] = jnp.zeros_like(pad_i)
    vec_col[my_c] = jnp.zeros((rhs, LANES), jnp.float32)
    for load in loads:
        load.wait()
    pad_f[0:3, 0:width] = vertices_ref[...]
    pad_i[0:4, 0:width] = connect_ref[...]
    pad_i[4:5, 0:width] = component_ref[...]
    vec_col[my_c, :, 0:width] = rhs_ref[...]
    vertices = pad_f[...]
    corners = [
        jnp.take_along_axis(
            vertices,
            jnp.broadcast_to(pad_i[k : k + 1, :], vertices.shape),
            axis=1,
            mode="promise_in_bounds",
        )
        for k in range(4)
    ]
    center, area = panel_frame(corners, pad_i[4:5, :], azimuth_ref[0], BLADES)
    size = jnp.sqrt(area[0] * area[0] + area[1] * area[1] + area[2] * area[2])
    frame = jnp.concatenate(
        center + [scale * part for part in area] + [jnp.zeros((2, LANES), jnp.float32)], axis=0
    )
    frames_col[my_c] = frame
    frames_row[my_r] = frame

    pl.semaphore_wait(barrier, nc - 1 + nr - 1)
    to_line(None, frames_row, sems_fr)
    to_plane(frames_col, sems_fc)
    to_plane(vec_col, sems_g)

    def at_slot(k, step, offset, length):
        start = k * step + offset
        return pl.ds(start if isinstance(start, int) else pl.multiple_of(start, SUB), length)

    def block_at(k):
        return lax.rem(my_c // 2 + k // 2, nc // 2) * 2 + k % 2

    def fill(k, c):
        columns = frames_col[c].T
        for s in range(LANES // SUB):
            x, y, z = (
                jnp.broadcast_to(columns[s * SUB : (s + 1) * SUB, k : k + 1], (SUB, LANES))
                for k in range(3)
            )
            place = at_slot(k, LANES, s * SUB, SUB)

            def one(r, carry):
                source = frames_row[r]
                dx, dy, dz = x - source[0:1], y - source[1:2], z - source[2:3]
                inverse = lax.rsqrt(dx * dx + dy * dy + (dz * dz + core_square))
                along = source[3:4] * dx + source[4:5] * dy + source[5:6] * dz
                value = inverse * (along * (inverse * inverse) + source[5:6])
                lead = value.astype(jnp.bfloat16)
                where = pl.ds(r * LANES if isinstance(r, int) else pl.multiple_of(r * LANES, LANES), LANES)
                matrix[0, place, where] = lead
                matrix[1, place, where] = (value - lead.astype(jnp.float32)).astype(jnp.bfloat16)
                return carry

            if nr <= 4:
                for r in range(nr):
                    one(r, 0)
            else:
                lax.fori_loop(0, nr, one, 0)

    def fill_step(k, carry):
        c = block_at(k)

        @pl.when(c != my_c)
        def _():
            arrived(frames_col, sems_fc, c)

        fill(k, c)
        return carry

    each_row(lambda r: arrived(frames_row, sems_fr, r))
    loop(0, nc, fill_step, 0)

    def lane_slot(k, length):
        start = k * LANES
        return pl.ds(start if isinstance(start, int) else pl.multiple_of(start, LANES), length)

    def product(ref, sems):
        def chip(k, total):
            for j in (0, 1):
                c = block_at(2 * k + j)

                @pl.when(c != my_c)
                def _():
                    arrived(ref, sems, c)

                halves[:, lane_slot(2 * k + j, LANES)] = split(ref[c])
            at = lane_slot(2 * k, 2 * LANES)
            part = jnp.dot(
                halves[:, at], matrix[0, at, :], preferred_element_type=jnp.float32
            ) + jnp.dot(halves[:, at], matrix[1, at, :], preferred_element_type=jnp.float32)
            return total + part

        total = jnp.zeros((2 * rhs, nr * LANES), jnp.float32)
        total = loop(0, nc // 2, chip, total)
        return total[:rhs] + total[rhs:]

    def apply_matrix(ref, sems_ref, send, recv, sems, beside=None):
        total = product(ref, sems_ref)
        for r in range(nr):
            send[r] = total[:, r * LANES : (r + 1) * LANES]
        to_line(send, recv, sems)
        recv[my_r] = send[my_r]
        if beside is not None:
            beside()
        each_row(lambda r: arrived(recv, sems, r))
        return size * ref[my_c] + jnp.sum(recv[...], axis=0)

    w1 = apply_matrix(vec_col, sems_g, send_one, recv_one, sems_one)
    image_col[my_c] = w1
    to_plane(image_col, sems_w)
    g = vec_col[my_c]
    stride = LANES // 4
    across = lax.broadcasted_iota(jnp.int32, (rhs, LANES), 1) - lax.broadcasted_iota(
        jnp.int32, (rhs, LANES), 0
    )

    def as_row(products):
        tile = jnp.zeros((rhs, LANES), jnp.float32)
        for k, values in enumerate(products):
            tile = jnp.where(
                across == k * stride, jnp.sum(values, axis=1, keepdims=True), tile
            )
        return jnp.sum(tile, axis=0, keepdims=True)

    def fields(row):
        return [row[:, k * stride : k * stride + rhs] for k in range(3)]

    def plane_sums():
        def add(c, sums):
            u, v = vec_col[c], image_col[c]
            return sums[0] + u * u, sums[1] + u * v, sums[2] + v * v

        sums = (jnp.zeros((rhs, LANES), jnp.float32),) * 3
        total_row[my_r] = as_row(loop(0, nc, add, sums))
        to_line(None, total_row, sems_tr)

    w2 = apply_matrix(image_col, sems_w, send_two, recv_two, sems_two, plane_sums)

    total_col[my_c] = as_row((g * w2, w1 * w2, w2 * w2))
    to_plane(total_col, sems_tc)
    each_row(lambda r: arrived(total_row, sems_tr, r))
    early = jnp.sum(total_row[...], axis=0)
    each_col(lambda c: arrived(total_col, sems_tc, c))
    total_end[my_r] = jnp.sum(total_col[...], axis=0)
    to_line(None, total_end, sems_te)
    each_row(lambda r: arrived(total_end, sems_te, r))
    late = jnp.sum(total_end[...], axis=0)
    of_g, of_w1, residual = small_solve(*fields(early), *fields(late))
    residual_ref[...] = residual
    pad_f[0:1, 0:rhs] = of_g
    pad_f[1:2, 0:rhs] = of_w1
    factors = pad_f[...].T
    answer = factors[0:rhs, 0:1] * g + factors[0:rhs, 1:2] * w1
    solution_ref[...] = answer[:, 0:width]
    for each, finish in started:
        each(finish)


def on_device(nr, nc, vertices, connect, component, azimuth, adjoint_rhs):
    rhs, width = adjoint_rhs.shape
    vmem = pl.BlockSpec(memory_space=pltpu.VMEM)
    f32 = jnp.float32
    matrix_bytes = 2 * nc * nr * LANES * LANES * 2
    pair = lambda n: pltpu.SemaphoreType.DMA((2, n))
    answer, residual = pl.pallas_call(
        functools.partial(kernel, nr, nc, width, rhs),
        out_shape=(
            jax.ShapeDtypeStruct((rhs, width), f32),
            jax.ShapeDtypeStruct((1, rhs), f32),
        ),
        in_specs=[pl.BlockSpec(memory_space=pltpu.HBM)] * 5,
        out_specs=(vmem, vmem),
        scratch_shapes=[
            pltpu.SMEM((1,), f32),
            pltpu.VMEM((3, width), f32),
            pltpu.VMEM((4, width), jnp.int32),
            pltpu.VMEM((1, width), jnp.int32),
            pltpu.VMEM((rhs, width), f32),
            pltpu.SemaphoreType.DMA((5,)),
            pltpu.VMEM((8, LANES), f32),
            pltpu.VMEM((8, LANES), jnp.int32),
            pltpu.VMEM((nc, 8, LANES), f32),
            pltpu.VMEM((nr, 8, LANES), f32),
            pltpu.VMEM((nc, rhs, LANES), f32),
            pltpu.VMEM((nc, rhs, LANES), f32),
            pltpu.VMEM((2 * rhs, nc * LANES), jnp.bfloat16),
            pltpu.VMEM((2, nc * LANES, nr * LANES), jnp.bfloat16),
            pltpu.VMEM((nr, rhs, LANES), f32),
            pltpu.VMEM((nr, rhs, LANES), f32),
            pltpu.VMEM((nr, rhs, LANES), f32),
            pltpu.VMEM((nr, rhs, LANES), f32),
            pltpu.VMEM((nr, 1, LANES), f32),
            pltpu.VMEM((nc, 1, LANES), f32),
            pltpu.VMEM((nr, 1, LANES), f32),
            pair(nc), pair(nr), pair(nc), pair(nc), pair(nr), pair(nr), pair(nr), pair(nc), pair(nr),
        ],
        compiler_params=pltpu.CompilerParams(
            collective_id=0,
            has_side_effects=True,
            vmem_limit_bytes=matrix_bytes + 20 * 1024 * 1024,
        ),
        cost_estimate=pl.CostEstimate(
            flops=2 * matrix_bytes * rhs, bytes_accessed=4 * rhs * width * 3, transcendentals=0
        ),
    )(azimuth, *(pltpu.with_memory_space_constraint(x, pltpu.HBM) for x in (vertices, connect, component.reshape(1, width), adjoint_rhs)))
    return answer, residual.reshape(rhs)


def solution(mesh):
    in_specs = (
        P(None, ("row", "col")),
        P(None, ("row", "col")),
        P(("row", "col")),
        P(),
        P(None, ("row", "col")),
    )
    out_specs = (P(None, ("row", "col")), P())
    return jax.shard_map(
        functools.partial(on_device, mesh.shape["row"], mesh.shape["col"]),
        mesh=mesh,
        in_specs=in_specs,
        out_specs=out_specs,
        check_vma=False,
    )
```
